32 devices in a mesh: seq: 8 (over y, x, core), head: 4 (over z).
Axes of the slice: x: 2, y: 2, z: 4, core: 2. Of those that a mesh axis runs over, the one named last changes fastest.
Arguments:
- queries: bfloat16 [1, 2048, 4096], P(None, 'seq', 'head'), may hold values from -6 to 6
- keys: bfloat16 [1, 2048, 4096], P(None, 'seq', 'head'), may hold values from -6 to 6
- values: bfloat16 [1, 2048, 4096], P(None, 'seq', 'head'), may hold values from -6 to 6
- out_weight: bfloat16 [4096, 4096], P('head'), may hold values from -0.09375 to 0.09375
- out_grad: bfloat16 [1, 2048, 4096], P(None, 'seq', 'head'), may hold values from -6 to 6
- block_doc: int32 [1, 8], replicated, may hold values from 0 to 2, never falling along the last dimension, each value on 1 to 6 neighbouring positions
Outputs:
- context: bfloat16 [1, 2048, 4096], P(None, 'seq', 'head')
- query_grad: bfloat16 [1, 2048, 4096], P(None, 'seq', 'head')
- key_grad: bfloat16 [1, 2048, 4096], P(None, 'seq', 'head')
- value_grad: bfloat16 [1, 2048, 4096], P(None, 'seq', 'head')
- weight_grad: bfloat16 [4096, 4096], P('head', 'seq')
The draws below stay inside these ranges and needn't reach their ends.
Inputs may be any that keep to these rules, and one draw needn't show every extreme that they name: `block_doc`: document numbers never fall along a pack, every document holds whole leaf blocks, and one document covers exactly 6 blocks.
All inputs are finite; a program needn't handle non-finite values.
Results may differ from the reference program's by a relative error of at most 0.019.
Values may be sent and summed in bfloat16 or wider, within the bound.
A program may use at most 128 MiB of HBM per device.

```python
import math
import jax
import jax.numpy as jnp
import numpy as np
from jax import lax

D = 4096
H = 32
DH = 128
LEAF = 256
BATCH = 1
HD = 4096
NBLK = 8
TOKENS = 2048
LEVELS = 3


def drawn_pair(key):
    shape = (BATCH, NBLK, LEAF, H, DH)
    query_all = jnp.clip(jax.random.normal(jax.random.fold_in(key, 21), shape, jnp.float32), -4.0, 4.0)
    key_all = jnp.clip(jax.random.normal(jax.random.fold_in(key, 22), shape, jnp.float32), -4.0, 4.0)
    return (query_all.reshape(BATCH, TOKENS, H * DH), key_all.reshape(BATCH, TOKENS, H * DH))


def draw_queries(key, part):
    return drawn_pair(key)[0].astype(jnp.bfloat16)


def draw_keys(key, part):
    return drawn_pair(key)[1].astype(jnp.bfloat16)


def spiked(values, key, source, target, blocks, factor):
    owner, partner = [(jnp.arange(values.shape[position]) // (values.shape[position] // blocks)).reshape([-1 if axis == position else 1 for axis in range(values.ndim)]) for position in (source, target)]
    chosen = jax.random.permutation(key, blocks)[partner]
    strong = (owner == chosen) | (owner == (partner + blocks // 2) % blocks)
    return jnp.where(strong, factor * values, values)


def block_levels(rng, shape, pieces, low, top_value):
    level = 1.0
    for dim, shards_of in pieces:
        steps = jax.random.uniform(jax.random.fold_in(jax.random.fold_in(rng, 6), dim), (shards_of,), jnp.float32, low / len(pieces), top_value / len(pieces))
        level = level * jnp.repeat(jnp.exp(steps), shape[dim] // shards_of).reshape((-1,) + (1,) * (len(shape) - 1 - dim))
    return level


def profile(count, total, most, skew):
    loads = [(1 << 20) // math.isqrt(grade ** skew) + 1 for grade in range(2, count + 1)]
    surplus, counts = total - most - (count - 1), [1] * (count - 1)
    while surplus > 0:
        candidates = [i for i in range(count - 1) if counts[i] < most]
        pool, budget = sum([loads[i] for i in candidates]), surplus
        for i in candidates:
            more = min(most - counts[i], max(1, budget * loads[i] // pool), surplus)
            counts[i] = counts[i] + more
            surplus = surplus - more
    return np.array([most] + counts)


def ragged_sizes(stream_key, amount, total, bound, lean):
    if amount == 2:
        one = jax.random.randint(stream_key, (), max(1, total - bound), min(bound, total - 1) + 1)
        return jnp.stack([one, total - one])
    lengths = jnp.asarray(profile(amount, total, bound, lean), jnp.int32)
    couples = (amount - 1) // 2
    donor, receiver = lengths[1:1 + 2 * couples:2], lengths[2:2 + 2 * couples:2]
    room = jnp.minimum(donor - 1, bound - receiver)
    passed = jax.random.randint(jax.random.fold_in(stream_key, 1), (couples,), 0, 1 << 20) % (room + 1)
    lengths = lengths.at[1:1 + 2 * couples:2].set(donor - passed).at[2:2 + 2 * couples:2].set(receiver + passed)
    return lengths[jax.random.permutation(jax.random.fold_in(stream_key, 2), amount)]


def bell_draw(rng, shape, spread, most, shards=(), held_as=jnp.bfloat16):
    values = spread * jax.random.normal(rng, shape, jnp.float32)
    if shards:
        values = values * block_levels(rng, shape, shards, -0.22, 0.18)
    return jnp.clip(values, -most, most).astype(held_as)


def heavy_noise(rng, dims, spread, limit, shards, heavy, kind=jnp.bfloat16):
    values = spread * jax.random.normal(rng, dims, jnp.float32)
    if shards:
        values = values * block_levels(rng, dims, shards, -0.22, 0.18)
    return jnp.clip(spiked(values, jax.random.fold_in(rng, 3), *heavy), -limit, limit).astype(kind)


def setup_inputs(seed: int = 0) -> dict:
    streams_of = jax.random.split(jax.random.key(seed), 7)
    queries = draw_queries(jax.random.fold_in(streams_of[6], 71), 0)
    keys = draw_keys(jax.random.fold_in(streams_of[6], 71), 0)
    values = bell_draw(streams_of[2], (BATCH, TOKENS, HD), 1.0, 6.0, ((1, 8), (2, 4)))
    out_weight = bell_draw(streams_of[3], (HD, D), HD ** -0.5, 0.09375, ((0, 4),))
    out_grad = heavy_noise(streams_of[4], (BATCH, TOKENS, D), 1.0, 6.0, ((1, 8), (2, 4)), (1, 2, 8, 2.0))
    block_doc = jax.vmap(lambda own: jnp.searchsorted(jnp.cumsum(ragged_sizes(own, 3, NBLK, 3 * NBLK // 4, 0)), jnp.arange(NBLK), side="right"))(jax.random.split(streams_of[5], BATCH)).reshape((BATCH, NBLK)).astype(jnp.int32)
    return dict(queries=queries, keys=keys, values=values, out_weight=out_weight, out_grad=out_grad, block_doc=block_doc)


def pool_pairs(blocks):
    pack_count, row_count, features = blocks.shape
    paired = blocks.reshape(pack_count, row_count // 2, 2, features).astype(jnp.float32)
    return ((paired[:, :, 0] + paired[:, :, 1]) * 0.5).astype(jnp.bfloat16)

def spread_pairs(gradient):
    pack_count, row_count, features = gradient.shape
    halved = gradient * 0.5
    return jnp.broadcast_to(halved[:, :, None, :], (pack_count, row_count, 2, features)).reshape(pack_count, 2 * row_count, features)

def round_half(array):
    return lax.optimization_barrier(array.astype(jnp.bfloat16)).astype(jnp.float32)

def add_rows(running, addend, row_start):
    current = lax.dynamic_slice_in_dim(running, row_start, addend.shape[1], 1)
    return lax.dynamic_update_slice_in_dim(running, current + addend, row_start, 1)

def reference(queries, keys, values, out_weight, out_grad, block_doc):
    scaling = 1.0 / math.sqrt(DH)
    columns = LEAF * (LEVELS + 1)
    key_levels = [keys]
    value_levels = [values]
    for level_num in range(1, LEVELS):
        key_levels.append(pool_pairs(key_levels[-1]))
        value_levels.append(pool_pairs(value_levels[-1]))
    context_grad_all = jnp.einsum('btk,hk->bth', out_grad.astype(jnp.float32), out_weight.astype(jnp.float32)).astype(jnp.bfloat16)
    weight_parts = [jnp.ones((2 * LEAF,), jnp.float32)]
    for level_num in range(1, LEVELS):
        weight_parts.append(jnp.full((LEAF,), 2.0 ** level_num, jnp.float32))
    col_weight = jnp.concatenate(weight_parts)
    leaf_iota = jnp.arange(LEAF, dtype=jnp.int32)

    def block_step(carry, block_num):
        key_grads, value_grads, weight_sum = carry
        partner = block_num ^ 1
        row_start = (block_num * LEAF).astype(jnp.int32)
        partner_start = (partner * LEAF).astype(jnp.int32)
        query_block = lax.dynamic_slice_in_dim(queries, row_start, LEAF, 1)
        key_parts = [lax.dynamic_slice_in_dim(keys, row_start, LEAF, 1), lax.dynamic_slice_in_dim(keys, partner_start, LEAF, 1)]
        value_parts = [lax.dynamic_slice_in_dim(values, row_start, LEAF, 1), lax.dynamic_slice_in_dim(values, partner_start, LEAF, 1)]
        block_parts = [jnp.full((LEAF,), block_num, jnp.int32), jnp.full((LEAF,), partner, jnp.int32)]
        level_starts = [row_start, partner_start]
        for level_num in range(1, LEVELS):
            sibling = block_num >> level_num ^ 1
            sib_start = (sibling * LEAF).astype(jnp.int32)
            level_starts.append(sib_start)
            key_parts.append(lax.dynamic_slice_in_dim(key_levels[level_num], sib_start, LEAF, 1))
            value_parts.append(lax.dynamic_slice_in_dim(value_levels[level_num], sib_start, LEAF, 1))
            block_parts.append((sibling << level_num) + leaf_iota // (LEAF >> level_num))
        key_cols = jnp.concatenate(key_parts, axis=1).astype(jnp.float32).reshape(BATCH, columns, H, DH)
        value_cols = jnp.concatenate(value_parts, axis=1).astype(jnp.float32).reshape(BATCH, columns, H, DH)
        col_block = jnp.concatenate(block_parts)
        col_doc = jnp.take(block_doc, col_block, axis=1)
        own_doc = lax.dynamic_slice_in_dim(block_doc, block_num, 1, 1)
        allowed = (col_doc == own_doc)[:, None, None, :]
        query_four = query_block.astype(jnp.float32).reshape(BATCH, LEAF, H, DH)
        scores = jnp.einsum('bthd,bchd->bhtc', query_four, key_cols) * scaling
        masked = jnp.where(allowed, scores, -jnp.inf)
        row_max = lax.optimization_barrier(jnp.max(masked, axis=-1, keepdims=True))
        weights = col_weight * jnp.exp(masked - row_max)
        prob_exact = weights / lax.optimization_barrier(jnp.sum(weights, axis=-1, keepdims=True))
        prob = round_half(prob_exact)
        context_four = round_half(jnp.einsum('bhtc,bchd->bthd', prob, value_cols))
        grad_four = lax.dynamic_slice_in_dim(context_grad_all, row_start, LEAF, 1).astype(jnp.float32).reshape(BATCH, LEAF, H, DH)
        row_delta = jnp.einsum('bthd,bthd->bht', grad_four, context_four)[..., None]
        prob_grad = jnp.einsum('bthd,bchd->bhtc', grad_four, value_cols)
        score_grad = round_half(prob_exact * (prob_grad - row_delta))
        query_grad_block = (jnp.einsum('bhtc,bchd->bthd', score_grad, key_cols) * scaling).astype(jnp.bfloat16).reshape(BATCH, LEAF, HD)
        key_col_grad = (jnp.einsum('bhtc,bthd->bchd', score_grad, query_four) * scaling).reshape(BATCH, columns, HD)
        value_col_grad = jnp.einsum('bhtc,bthd->bchd', prob, grad_four).reshape(BATCH, columns, HD)
        key_grads = list(key_grads)
        value_grads = list(value_grads)
        for piece_num in range(LEVELS + 1):
            level_num = max(piece_num - 1, 0)
            key_piece = key_col_grad[:, piece_num * LEAF:(piece_num + 1) * LEAF]
            value_piece = value_col_grad[:, piece_num * LEAF:(piece_num + 1) * LEAF]
            key_grads[level_num] = add_rows(key_grads[level_num], key_piece, level_starts[piece_num])
            value_grads[level_num] = add_rows(value_grads[level_num], value_piece, level_starts[piece_num])
        context_flat = context_four.reshape(BATCH, LEAF, HD)
        grad_block = lax.dynamic_slice_in_dim(out_grad, row_start, LEAF, 1).astype(jnp.float32)
        partial_block = round_half(jnp.einsum('bth,btk->hk', context_flat, grad_block))
        weight_sum = weight_sum + partial_block
        return ((tuple(key_grads), tuple(value_grads), weight_sum), (context_flat.astype(jnp.bfloat16), query_grad_block))
    zero_levels = tuple((jnp.zeros((BATCH, TOKENS >> level_num, HD), jnp.float32) for level_num in range(LEVELS)))
    start_carry = (zero_levels, zero_levels, jnp.zeros((HD, D), jnp.float32))
    carry, stacked = lax.scan(block_step, start_carry, jnp.arange(NBLK, dtype=jnp.int32))
    key_grads, value_grads, weight_sum = carry
    key_grads = list(key_grads)
    value_grads = list(value_grads)
    for level_num in range(LEVELS - 1, 0, -1):
        key_grads[level_num - 1] = key_grads[level_num - 1] + spread_pairs(key_grads[level_num])
        value_grads[level_num - 1] = value_grads[level_num - 1] + spread_pairs(value_grads[level_num])
    context = jnp.transpose(stacked[0], (1, 0, 2, 3)).reshape(BATCH, TOKENS, HD)
    query_grad = jnp.transpose(stacked[1], (1, 0, 2, 3)).reshape(BATCH, TOKENS, HD)
    return (context, query_grad, key_grads[0].astype(jnp.bfloat16), value_grads[0].astype(jnp.bfloat16), weight_sum.astype(jnp.bfloat16))
```

```python
import functools
import math

import jax
import jax.numpy as jnp
from jax import lax
from jax.experimental import pallas as pl
from jax.experimental.pallas import tpu as pltpu
from jax.sharding import PartitionSpec as P

DH = 128
GROUP_HEADS = 2
F32 = jnp.float32
BF16 = jnp.bfloat16


def flipped(index, mask):
    out = index
    bit = 1
    while bit <= mask:
        if mask & bit:
            out = out + (1 - 2 * lax.rem(lax.div(index, jnp.int32(bit)), jnp.int32(2))) * bit
        bit *= 2
    return out


def dot_nn(a, b):
    return lax.dot_general(a, b, (((1,), (0,)), ((), ())), preferred_element_type=F32)


def dot_nt(a, b):
    return lax.dot_general(a, b, (((1,), (1,)), ((), ())), preferred_element_type=F32)


def dot_tn(a, b):
    return lax.dot_general(a, b, (((0,), (0,)), ((), ())), preferred_element_type=F32)


def pieces_of(seq_count, leaf):
    rows, starts, at = {}, {}, 0
    for parity in (0, 1):
        for o in range(parity, seq_count, 2):
            level = max(o.bit_length() - 1, 0)
            rows[o], starts[o] = leaf >> level, at
            at += rows[o]
    return rows, starts, at


def kernel(seq_count, head_count, leaf, feats,
           doc, q_ref, k_ref, v_ref, og_ref, w_ref,
           ctx_out, dq_out, dk_out, dv_out, wg_out,
           wv, ogf, kc, pb, probs, ctxs, ogs, cga, cgt, own, dbuf, pair, back, acc,
           s_w, s_up, s_dn, r_z, s_kv, r_kv, s_a, r_a, s_c, r_c, s_p, r_p, s_g, r_g):
    me = lax.axis_index("seq")
    z = lax.axis_index("head")
    partner = flipped(me, 1)
    levels = seq_count.bit_length() - 1
    rows, starts, cols = pieces_of(seq_count, leaf)
    half = cols // 2
    heads = feats // DH
    gcols = GROUP_HEADS * DH
    groups = feats // gcols
    per_shard = seq_count // head_count
    kcols = feats // per_shard
    scaling = 1.0 / math.sqrt(DH)

    def remote(src, dst, send, recv, **where):
        return pltpu.make_async_remote_copy(
            src_ref=src, dst_ref=dst, send_sem=send, recv_sem=recv,
            device_id=where, device_id_type=pl.DeviceIdType.MESH)

    def arrived(dst, recv):
        remote(dst, dst, recv, recv, seq=partner).wait_recv()

    def w_copy(zp):
        return pltpu.make_async_copy(
            w_ref.at[:, pl.ds(zp * feats, feats)], wv.at[zp], s_w.at[zp])

    def up_copy(zp):
        return remote(ogf.at[zp], ogf.at[zp], s_up.at[zp], r_z.at[zp], head=z + 1)

    def down_copy(zp):
        return remote(ogf.at[zp], ogf.at[zp], s_dn.at[zp], r_z.at[zp], head=z - 1)

    def kv_copy(o):
        if o == 0:
            src, dst, to = kc.at[:, pl.ds(0, leaf)], 1, partner
        elif o % 2 == 0:
            level = o.bit_length() - 1
            src = pb.at[:, pl.ds(leaf - (leaf >> (level - 1)), rows[o])]
            dst, to = o, flipped(me, o)
        else:
            src, dst, to = kc.at[:, pl.ds(starts[o - 1], rows[o])], o, partner
        slot = kc.at[:, pl.ds(starts[dst], rows[dst])]
        return remote(src, slot, s_kv.at[o], r_kv.at[dst], seq=to)

    def kv_arrived(o):
        arrived(kc.at[:, pl.ds(starts[o], rows[o])], r_kv.at[o])

    def a_copy(zp, j):
        to = zp * per_shard + j
        return remote(ogf.at[zp, :, pl.ds(j * kcols, kcols)], ogs.at[me],
                      s_a.at[to], r_a.at[me], seq=to)

    def c_copy(o):
        if o == 1 or o % 2 == 0:
            return remote(ctxs.at[0], ctxs.at[o], s_c.at[o], r_c.at[o], seq=flipped(me, o))
        return remote(ctxs.at[o - 1], ctxs.at[o], s_c.at[o], r_c.at[o], seq=partner)

    def p_copy(g):
        return remote(dbuf.at[g, :, pl.ds(half, half)], pair.at[g], s_p.at[g], r_p.at[g],
                      seq=partner)

    def g_copy(g, o):
        return remote(dbuf.at[g, :, pl.ds(starts[o], rows[o])],
                      back.at[g, :, pl.ds(starts[o] - leaf, rows[o])],
                      s_g.at[g, o // 2], r_g.at[g, o // 2], seq=flipped(me, o))

    far = list(range(2, seq_count, 2))

    for zp in range(head_count):
        w_copy(zp).start()
    barrier = pltpu.get_barrier_semaphore()
    for o in range(1, seq_count):
        pl.semaphore_signal(barrier, inc=1, device_id={"seq": flipped(me, o)},
                            device_id_type=pl.DeviceIdType.MESH)

    @pl.when(z > 0)
    def _():
        pl.semaphore_signal(barrier, inc=1, device_id={"head": z - 1},
                            device_id_type=pl.DeviceIdType.MESH)

    @pl.when(z < head_count - 1)
    def _():
        pl.semaphore_signal(barrier, inc=1, device_id={"head": z + 1},
                            device_id_type=pl.DeviceIdType.MESH)

    ogf[z] = og_ref[...]
    kc[0, 0:leaf] = k_ref[...]
    kc[1, 0:leaf] = v_ref[...]
    for which, ref in enumerate((k_ref, v_ref)):
        for c in range(0, feats, 256):
            block = ref[:, c:c + 256]
            at = 0
            for level in range(1, levels):
                n = leaf >> level
                pool = jnp.where(
                    lax.broadcasted_iota(jnp.int32, (n, 2 * n), 1) // 2
                    == lax.broadcasted_iota(jnp.int32, (n, 2 * n), 0), 0.5, 0.0).astype(BF16)
                block = dot_nn(pool, block).astype(BF16)
                pb[which, at:at + n, c:c + 256] = block
                at += n
    inner = (z > 0) & (z < head_count - 1)

    @pl.when(inner)
    def _():
        pl.semaphore_wait(barrier, seq_count + 1)

    @pl.when(jnp.logical_not(inner))
    def _():
        pl.semaphore_wait(barrier, seq_count)

    @pl.when(z > 0)
    def _():
        down_copy(z).start()

    @pl.when(z < head_count - 1)
    def _():
        up_copy(z).start()

    kv_copy(0).start()
    for o in far:
        kv_copy(o).start()

    def scatter_grad(zp):
        for j in range(per_shard):
            @pl.when(zp * per_shard + j != me)
            def _():
                a_copy(zp, j).start()

            @pl.when(zp * per_shard + j == me)
            def _():
                ogs[me] = ogf[zp, :, j * kcols:(j + 1) * kcols]

    def project(zp, first=False):
        grad = ogf[zp]

        @pl.loop(0, feats // 256)
        def _(t):
            at = pl.ds(pl.multiple_of(t * 256, 256), 256)
            term = dot_nt(wv[zp, at], grad)
            cga[at] = term if first else cga[at] + term

    def gather_step(k):
        @pl.when(z >= k)
        def _():
            zp = z - k
            arrived(ogf.at[zp], r_z.at[zp])

            @pl.when(z < head_count - 1)
            def _():
                up_copy(zp).start()

        @pl.when(z + k < head_count)
        def _():
            zp = z + k
            arrived(ogf.at[zp], r_z.at[zp])

            @pl.when(z > 0)
            def _():
                down_copy(zp).start()

        @pl.when(z >= k)
        def _():
            scatter_grad(z - k)
            project(z - k)

        @pl.when(z + k < head_count)
        def _():
            scatter_grad(z + k)
            project(z + k)

    scatter_grad(z)
    for zp in range(head_count):
        w_copy(zp).wait()
    project(z, first=True)
    gather_step(1)

    for o in far:
        kv_arrived(o)
        kv_copy(o + 1).start()
    kv_arrived(1)
    for o in far:
        kv_arrived(o + 1)

    log2e = 1.4426950408889634
    my_doc = doc[0, me]
    biases = []
    for o in sorted(starts, key=lambda p: starts[p]):
        level = float(max(o.bit_length() - 1, 0))
        same = doc[0, flipped(me, o)] == my_doc
        biases.append((starts[o], rows[o], jnp.where(same, level, -1e30).astype(F32)))

    def forward(first, last):
        @pl.loop(first, last)
        def _(h):
            at = pl.ds(pl.multiple_of(h * DH, DH), DH)
            keys, vals, query = kc[0, :, at], kc[1, :, at], q_ref[:, at]
            raw = dot_nt(keys, query)
            shifted = jnp.concatenate(
                [raw[s:s + n] * (scaling * log2e) + b for s, n, b in biases], axis=0)
            top = jnp.max(shifted, axis=0, keepdims=True)
            weights = jnp.exp2(shifted - top)
            inv = 1.0 / jnp.sum(weights, axis=0, keepdims=True)
            prob = (weights * inv).astype(BF16)
            probs[h] = prob
            out = dot_tn(vals, prob)
            ctxs[0, at] = out.astype(BF16)
            ctx_out[:, at] = out.T.astype(BF16)

    forward(0, heads // 2)
    if head_count > 2:
        gather_step(2)
    forward(heads // 2, heads)
    for o in far + [1]:
        c_copy(o).start()
    for k in range(3, head_count):
        gather_step(k)
    cgt[...] = cga[...].astype(BF16)

    def finish(g):
        arrived(pair.at[g], r_p.at[g])
        for which in range(2):
            dbuf[g, which, leaf:half] = (
                dbuf[g, which, leaf:half].astype(F32) + pair[g, which, leaf:half].astype(F32)
            ).astype(BF16)
        for o in far:
            g_copy(g, o).start()

    @pl.loop(0, groups)
    def _(g):
        for i in range(GROUP_HEADS):
            h = g * GROUP_HEADS + i
            at = pl.ds(pl.multiple_of(h * DH, DH), DH)
            lanes = slice(i * DH, (i + 1) * DH)
            keys, vals, query = kc[0, :, at], kc[1, :, at], q_ref[:, at]
            grad = cgt[at]
            prob = probs[h]
            delta = jnp.sum(grad.astype(F32) * ctxs[0, at].astype(F32), axis=0, keepdims=True)
            prob_grad = dot_nn(vals, grad)
            score_grad = (prob.astype(F32) * (prob_grad - delta)).astype(BF16)
            dq_out[:, at] = (dot_tn(keys, score_grad) * scaling).T.astype(BF16)
            dk = dot_nn(score_grad, query) * scaling
            dv = dot_nt(prob, grad)
            for which, full in enumerate((dk, dv)):
                own[g, which, :, lanes] = full[:leaf]
                dbuf[g, which, leaf:, lanes] = full[leaf:].astype(BF16)
        p_copy(g).start()

        @pl.when(g > 0)
        def _():
            finish(g - 1)

    finish(groups - 1)

    for o in far:
        arrived(ctxs.at[o], r_c.at[o])
        c_copy(o + 1).start()
    for n, o in enumerate([0, 1] + far + [o + 1 for o in far]):
        if o % 2 == 1:
            arrived(ctxs.at[o], r_c.at[o])
        src = flipped(me, o)
        if o:
            arrived(ogs.at[src], r_a.at[src])
        grad = ogs[src]

        @pl.loop(0, feats // 256)
        def _(t):
            at = pl.ds(pl.multiple_of(t * 256, 256), 256)
            term = dot_nn(ctxs[o, at], grad)
            acc[at] = term if n == 0 else acc[at] + term

    wg_out[...] = acc[...].astype(BF16)

    far_rows = half - leaf
    r_id = lax.broadcasted_iota(jnp.int32, (leaf, far_rows), 0)
    c_id = lax.broadcasted_iota(jnp.int32, (leaf, far_rows), 1)
    spread = jnp.zeros((leaf, far_rows), F32)
    for o in far:
        level = o.bit_length() - 1
        hit = (lax.shift_right_logical(r_id, level) == c_id - (starts[o] - leaf))
        spread = jnp.where(hit, 0.5 ** level, spread)
    spread = spread.astype(BF16)
    for g in range(groups):
        for o in far:
            arrived(back.at[g, :, pl.ds(starts[o] - leaf, rows[o])], r_g.at[g, o // 2])
        for which, out in enumerate((dk_out, dv_out)):
            total = own[g, which] + pair[g, which, :leaf].astype(F32) + dot_nn(
                spread, back[g, which])
            out[:, g * gcols:(g + 1) * gcols] = total.astype(BF16)

    for zp in range(head_count):
        @pl.when((z < head_count - 1) & (zp <= z))
        def _():
            up_copy(zp).wait_send()

        @pl.when((z > 0) & (zp >= z))
        def _():
            down_copy(zp).wait_send()

        for j in range(per_shard):
            @pl.when(zp * per_shard + j != me)
            def _():
                a_copy(zp, j).wait_send()
    kv_copy(0).wait_send()
    for o in far:
        kv_copy(o).wait_send()
        kv_copy(o + 1).wait_send()
    for o in range(1, seq_count):
        c_copy(o).wait_send()
    for g in range(groups):
        p_copy(g).wait_send()
        for o in far:
            g_copy(g, o).wait_send()


def local(queries, keys, values, out_weight, out_grad, block_doc):
    seq_count, head_count = lax.axis_size("seq"), lax.axis_size("head")
    _, leaf, feats = queries.shape
    model = out_weight.shape[1]
    _, _, cols = pieces_of(seq_count, leaf)
    half = cols // 2
    heads = feats // DH
    gcols = GROUP_HEADS * DH
    groups = feats // gcols
    kcols = model // seq_count
    dma = pltpu.SemaphoreType.DMA
    vmem = pl.BlockSpec(memory_space=pltpu.VMEM)
    block = jax.ShapeDtypeStruct((leaf, feats), BF16)
    results = pl.pallas_call(
        functools.partial(kernel, seq_count, head_count, leaf, feats),
        out_shape=[block] * 4 + [jax.ShapeDtypeStruct((feats, kcols), BF16)],
        in_specs=[pl.BlockSpec(memory_space=pltpu.SMEM)] + [vmem] * 4
        + [pl.BlockSpec(memory_space=pl.ANY)],
        out_specs=[vmem] * 5,
        scratch_shapes=[
            pltpu.VMEM((head_count, feats, feats), BF16),
            pltpu.VMEM((head_count, leaf, feats), BF16),
            pltpu.VMEM((2, cols, feats), BF16),
            pltpu.VMEM((2, leaf, feats), BF16),
            pltpu.VMEM((heads, cols, leaf), BF16),
            pltpu.VMEM((seq_count, feats, leaf), BF16),
            pltpu.VMEM((seq_count, leaf, kcols), BF16),
            pltpu.VMEM((feats, leaf), F32),
            pltpu.VMEM((feats, leaf), BF16),
            pltpu.VMEM((groups, 2, leaf, gcols), F32),
            pltpu.VMEM((groups, 2, cols, gcols), BF16),
            pltpu.VMEM((groups, 2, half, gcols), BF16),
            pltpu.VMEM((groups, 2, half - leaf, gcols), BF16),
            pltpu.VMEM((feats, kcols), F32),
            dma((head_count,)), dma((head_count,)), dma((head_count,)), dma((head_count,)),
            dma((seq_count,)), dma((seq_count,)), dma((seq_count,)), dma((seq_count,)),
            dma((seq_count,)), dma((seq_count,)), dma((groups,)), dma((groups,)),
            dma((groups, seq_count // 2)), dma((groups, seq_count // 2)),
        ],
        compiler_params=pltpu.CompilerParams(
            collective_id=0, has_side_effects=True, vmem_limit_bytes=60 * 1024 * 1024),
        cost_estimate=pl.CostEstimate(
            flops=8 * 10**9, bytes_accessed=16 * 2**20, transcendentals=2 * 2**20),
        name="hier_attention",
    )(block_doc, queries[0], keys[0], values[0], out_grad[0], out_weight)
    context, query_grad, key_grad, value_grad, weight_grad = results
    return context[None], query_grad[None], key_grad[None], value_grad[None], weight_grad


def solution(mesh):
    blocks = P(None, "seq", "head")
    return jax.shard_map(
        local,
        mesh=mesh,
        in_specs=(blocks, blocks, blocks, P("head", None), blocks, P()),
        out_specs=(blocks, blocks, blocks, blocks, P("head", "seq")),
        check_vma=False,
    )
```

```python
import functools
import math

import jax
import jax.numpy as jnp
from jax import lax
from jax.experimental import pallas as pl
from jax.experimental.pallas import tpu as pltpu
from jax.sharding import PartitionSpec as P

DH = 128
GROUP_HEADS = 2
F32 = jnp.float32
BF16 = jnp.bfloat16


def flipped(index, mask):
    out = index
    bit = 1
    while bit <= mask:
        if mask & bit:
            out = out + (1 - 2 * lax.rem(lax.div(index, jnp.int32(bit)), jnp.int32(2))) * bit
        bit *= 2
    return out


def top_bit(o):
    return 1 << (o.bit_length() - 1)


def dot_nn(a, b):
    return lax.dot_general(a, b, (((1,), (0,)), ((), ())), preferred_element_type=F32)


def dot_nt(a, b):
    return lax.dot_general(a, b, (((1,), (1,)), ((), ())), preferred_element_type=F32)


def dot_tn(a, b):
    return lax.dot_general(a, b, (((0,), (0,)), ((), ())), preferred_element_type=F32)


def pieces_of(seq_count, leaf):
    rows, starts, at = {}, {}, 0
    for parity in (0, 1):
        for o in range(parity, seq_count, 2):
            level = max(o.bit_length() - 1, 0)
            rows[o], starts[o] = leaf >> level, at
            at += rows[o]
    return rows, starts, at


def kernel(seq_count, head_count, leaf, feats,
           doc, q_ref, k_ref, v_ref, og_ref, w_ref,
           ctx_out, dq_out, dk_out, dv_out, wg_out,
           wv, ogf, kc, pb, probs, ctxs, ogs, cga, cgt, own, dbuf, pair, back, acc,
           s_w, s_up, s_dn, r_z, s_kv, r_kv, s_a, r_a, s_c, r_c, s_p, r_p, s_g, r_g):
    me = lax.axis_index("seq")
    z = lax.axis_index("head")
    partner = flipped(me, 1)
    levels = seq_count.bit_length() - 1
    rows, starts, cols = pieces_of(seq_count, leaf)
    half = cols // 2
    heads = feats // DH
    gcols = GROUP_HEADS * DH
    groups = feats // gcols
    per_shard = seq_count // head_count
    kcols = feats // per_shard
    scaling = 1.0 / math.sqrt(DH)

    def remote(src, dst, send, recv, **where):
        return pltpu.make_async_remote_copy(
            src_ref=src, dst_ref=dst, send_sem=send, recv_sem=recv,
            device_id=where, device_id_type=pl.DeviceIdType.MESH)

    def arrived(dst, recv):
        remote(dst, dst, recv, recv, seq=partner).wait_recv()

    def w_copy(zp):
        return pltpu.make_async_copy(
            w_ref.at[:, pl.ds(zp * feats, feats)], wv.at[zp], s_w.at[zp])

    def up_copy(zp):
        return remote(ogf.at[zp], ogf.at[zp], s_up.at[zp], r_z.at[zp], head=z + 1)

    def down_copy(zp):
        return remote(ogf.at[zp], ogf.at[zp], s_dn.at[zp], r_z.at[zp], head=z - 1)

    def kv_copy(o):
        if o == 0:
            src, dst, to = kc.at[:, pl.ds(0, leaf)], 1, partner
        elif o % 2 == 0:
            src = pb.at[:, pl.ds(starts[o] - leaf, rows[o])]
            dst, to = o, flipped(me, top_bit(o))
        else:
            src, dst, to = kc.at[:, pl.ds(starts[o - 1], rows[o])], o, partner
        slot = kc.at[:, pl.ds(starts[dst], rows[dst])]
        return remote(src, slot, s_kv.at[o], r_kv.at[dst], seq=to)

    def kv_arrived(o):
        arrived(kc.at[:, pl.ds(starts[o], rows[o])], r_kv.at[o])

    def a_copy(zp, j):
        to = zp * per_shard + j
        return remote(ogf.at[zp, :, pl.ds(j * kcols, kcols)], ogs.at[me],
                      s_a.at[to], r_a.at[me], seq=to)

    def c_parts(o):
        return 1 if o % 2 == 1 or o == top_bit(o) else 2

    def c_copy(o, n=0):
        if o == top_bit(o):
            src, dst, bit = ctxs.at[0], ctxs.at[o], o
        elif o % 2 == 1:
            src, dst, bit = ctxs.at[o - 1], ctxs.at[o], 1
        else:
            bit = o & -o if n else top_bit(o)
            part = pl.ds(n * (feats // 2), feats // 2)
            src, dst = ctxs.at[o ^ bit, part], ctxs.at[o, part]
        return remote(src, dst, s_c.at[o, n], r_c.at[o, n], seq=flipped(me, bit))

    def c_arrived(o):
        for n in range(c_parts(o)):
            c_copy(o, n).wait_recv()

    def p_copy(g):
        return remote(dbuf.at[g, :, pl.ds(half, half)], pair.at[g], s_p.at[g], r_p.at[g],
                      seq=partner)

    def level_rows(level):
        return starts[1 << level], (leaf >> level) << (level - 1)

    def g_copy(g, level):
        at, n = level_rows(level)
        return remote(dbuf.at[g, :, pl.ds(at, n)], back.at[g, level - 1],
                      s_g.at[g, level - 1], r_g.at[g, level - 1], seq=flipped(me, 1 << level))

    far = list(range(2, seq_count, 2))

    for zp in range(head_count):
        w_copy(zp).start()
    barrier = pltpu.get_barrier_semaphore()
    for o in range(1, seq_count):
        pl.semaphore_signal(barrier, inc=1, device_id={"seq": flipped(me, o)},
                            device_id_type=pl.DeviceIdType.MESH)

    @pl.when(z > 0)
    def _():
        pl.semaphore_signal(barrier, inc=1, device_id={"head": z - 1},
                            device_id_type=pl.DeviceIdType.MESH)

    @pl.when(z < head_count - 1)
    def _():
        pl.semaphore_signal(barrier, inc=1, device_id={"head": z + 1},
                            device_id_type=pl.DeviceIdType.MESH)

    ogf[z] = og_ref[...]
    kc[0, 0:leaf] = k_ref[...]
    kc[1, 0:leaf] = v_ref[...]

    def pool_from(source, low, r):
        for which in range(2):
            for c in range(0, feats, 256):
                piece = source(which, c)
                for level in range(low + 1, levels):
                    n = leaf >> level
                    pool = jnp.where(
                        lax.shift_right_logical(
                            lax.broadcasted_iota(jnp.int32, (n, 2 * n), 1), 1)
                        == lax.broadcasted_iota(jnp.int32, (n, 2 * n), 0), 0.5, 0.0).astype(BF16)
                    piece = dot_nn(pool, piece).astype(BF16)
                    at = starts[(1 << level) + r] - leaf
                    pb[which, at:at + n, c:c + 256] = piece

    pool_from(lambda which, c: (k_ref, v_ref)[which][:, c:c + 256], 0, 0)
    inner = (z > 0) & (z < head_count - 1)

    @pl.when(inner)
    def _():
        pl.semaphore_wait(barrier, seq_count + 1)

    @pl.when(jnp.logical_not(inner))
    def _():
        pl.semaphore_wait(barrier, seq_count)

    @pl.when(z > 0)
    def _():
        down_copy(z).start()

    @pl.when(z < head_count - 1)
    def _():
        up_copy(z).start()

    kv_copy(0).start()
    for level in range(1, levels):
        kv_copy(1 << level).start()

    def scatter_grad(zp):
        for j in range(per_shard):
            @pl.when(zp * per_shard + j != me)
            def _():
                a_copy(zp, j).start()

            @pl.when(zp * per_shard + j == me)
            def _():
                ogs[me] = ogf[zp, :, j * kcols:(j + 1) * kcols]

    def project(zp, first=False):
        grad = ogf[zp]

        @pl.loop(0, feats // 256)
        def _(t):
            at = pl.ds(pl.multiple_of(t * 256, 256), 256)
            term = dot_nt(wv[zp, at], grad)
            cga[at] = term if first else cga[at] + term

    def gather_step(k):
        @pl.when(z >= k)
        def _():
            zp = z - k
            arrived(ogf.at[zp], r_z.at[zp])

            @pl.when(z < head_count - 1)
            def _():
                up_copy(zp).start()

        @pl.when(z + k < head_count)
        def _():
            zp = z + k
            arrived(ogf.at[zp], r_z.at[zp])

            @pl.when(z > 0)
            def _():
                down_copy(zp).start()

        @pl.when(z >= k)
        def _():
            scatter_grad(z - k)
            project(z - k)

        @pl.when(z + k < head_count)
        def _():
            scatter_grad(z + k)
            project(z + k)

    scatter_grad(z)
    for zp in range(head_count):
        w_copy(zp).wait()
    project(z, first=True)
    gather_step(1)

    for o in far:
        kv_arrived(o)
        kv_copy(o + 1).start()
        low = o.bit_length() - 1
        if low + 1 < levels:
            pool_from(lambda which, c: kc[which, starts[o]:starts[o] + rows[o], c:c + 256],
                      low, o)
            for level in range(low + 1, levels):
                kv_copy((1 << level) + o).start()
    kv_arrived(1)
    for o in far:
        kv_arrived(o + 1)

    log2e = 1.4426950408889634
    my_doc = doc[0, me]
    biases = []
    for o in sorted(starts, key=lambda p: starts[p]):
        level = float(max(o.bit_length() - 1, 0))
        same = doc[0, flipped(me, o)] == my_doc
        biases.append((starts[o], rows[o], jnp.where(same, level, -1e30).astype(F32)))

    def forward(first, last):
        @pl.loop(first, last)
        def _(h):
            at = pl.ds(pl.multiple_of(h * DH, DH), DH)
            keys, vals, query = kc[0, :, at], kc[1, :, at], q_ref[:, at]
            raw = dot_nt(keys, query)
            shifted = jnp.concatenate(
                [raw[s:s + n] * (scaling * log2e) + b for s, n, b in biases], axis=0)
            top = jnp.max(shifted, axis=0, keepdims=True)
            weights = jnp.exp2(shifted - top)
            inv = 1.0 / jnp.sum(weights, axis=0, keepdims=True)
            prob = (weights * inv).astype(BF16)
            probs[h] = prob
            out = dot_tn(vals, prob)
            ctxs[0, at] = out.astype(BF16)
            ctx_out[:, at] = out.T.astype(BF16)

    forward(0, heads // 2)
    if head_count > 2:
        gather_step(2)
    forward(heads // 2, heads)
    for level in range(levels - 1, -1, -1):
        c_copy(1 << level).start()
    for k in range(3, head_count):
        gather_step(k)
    cgt[...] = cga[...].astype(BF16)

    def spread_from(level):
        at, n = level_rows(level)
        row = lax.broadcasted_iota(jnp.int32, (at, n), 0)
        col = lax.broadcasted_iota(jnp.int32, (at, n), 1)
        out = jnp.zeros((at, n), F32)
        for r in range(0, 1 << level, 2):
            low = max(r.bit_length() - 1, 0)
            first = starts[(1 << level) + r] - at
            inside = (row >= starts[r]) & (row < starts[r] + rows[r])
            hit = lax.shift_right_logical(row - starts[r], level - low) == col - first
            out = jnp.where(inside & hit, 0.5 ** (level - low), out)
        return out.astype(BF16)

    def finish_pair(g):
        arrived(pair.at[g], r_p.at[g])
        for which in range(2):
            own[g, which] += pair[g, which, :leaf].astype(F32)
            dbuf[g, which, leaf:half] = (
                dbuf[g, which, leaf:half].astype(F32) + pair[g, which, leaf:half].astype(F32)
            ).astype(BF16)
        g_copy(g, levels - 1).start()

    def finish_level(g, level, spread):
        at, n = level_rows(level)
        arrived(back.at[g, level - 1], r_g.at[g, level - 1])
        for which in range(2):
            more = dot_nn(spread, back[g, level - 1, which])
            own[g, which] += more[:leaf]
            if at > leaf:
                dbuf[g, which, leaf:at] = (
                    dbuf[g, which, leaf:at].astype(F32) + more[leaf:]).astype(BF16)
        if level > 1:
            g_copy(g, level - 1).start()

    @pl.loop(0, groups)
    def _(g):
        for i in range(GROUP_HEADS):
            h = g * GROUP_HEADS + i
            at = pl.ds(pl.multiple_of(h * DH, DH), DH)
            lanes = slice(i * DH, (i + 1) * DH)
            keys, vals, query = kc[0, :, at], kc[1, :, at], q_ref[:, at]
            grad = cgt[at]
            prob = probs[h]
            delta = jnp.sum(grad.astype(F32) * ctxs[0, at].astype(F32), axis=0, keepdims=True)
            prob_grad = dot_nn(vals, grad)
            score_grad = (prob.astype(F32) * (prob_grad - delta)).astype(BF16)
            dq_out[:, at] = (dot_tn(keys, score_grad) * scaling).T.astype(BF16)
            dk = dot_nn(score_grad, query) * scaling
            dv = dot_nt(prob, grad)
            for which, full in enumerate((dk, dv)):
                own[g, which, :, lanes] = full[:leaf]
                dbuf[g, which, leaf:, lanes] = full[leaf:].astype(BF16)
        p_copy(g).start()

        @pl.when(g > 0)
        def _():
            finish_pair(g - 1)

    finish_pair(groups - 1)
    for level in range(levels - 1, 1, -1):
        spread = spread_from(level)

        @pl.loop(0, groups)
        def _(g):
            finish_level(g, level, spread)

    def add_weight(o, first=False):
        src = flipped(me, o)
        if o:
            arrived(ogs.at[src], r_a.at[src])
        grad = ogs[src]

        @pl.loop(0, feats // 256)
        def _(t):
            at = pl.ds(pl.multiple_of(t * 256, 256), 256)
            term = dot_nn(ctxs[o, at], grad)
            acc[at] = term if first else acc[at] + term

    for o in far:
        c_arrived(o)
        c_copy(o + 1).start()
        for level in range(1, levels):
            bit = 1 << level
            if o & bit:
                continue
            to = o | bit
            if bit == top_bit(to):
                c_copy(to, 0).start()
            if bit == to & -to:
                c_copy(to, 1).start()
    add_weight(0, first=True)
    c_arrived(1)
    add_weight(1)
    for o in far:
        add_weight(o)
        c_arrived(o + 1)
        add_weight(o + 1)

    wg_out[...] = acc[...].astype(BF16)

    last = spread_from(1)
    for g in range(groups):
        finish_level(g, 1, last)
        for which, out in enumerate((dk_out, dv_out)):
            out[:, g * gcols:(g + 1) * gcols] = own[g, which].astype(BF16)

    for zp in range(head_count):
        @pl.when((z < head_count - 1) & (zp <= z))
        def _():
            up_copy(zp).wait_send()

        @pl.when((z > 0) & (zp >= z))
        def _():
            down_copy(zp).wait_send()

        for j in range(per_shard):
            @pl.when(zp * per_shard + j != me)
            def _():
                a_copy(zp, j).wait_send()
    kv_copy(0).wait_send()
    for o in far:
        kv_copy(o).wait_send()
        kv_copy(o + 1).wait_send()
    for o in range(1, seq_count):
        for n in range(c_parts(o)):
            c_copy(o, n).wait_send()
    for g in range(groups):
        p_copy(g).wait_send()
        for level in range(1, levels):
            g_copy(g, level).wait_send()


def copy_kernel(*refs):
    count = len(refs) // 2
    sems = refs[-1]
    copies = [pltpu.make_async_copy(refs[i], refs[count + i], sems.at[i]) for i in range(count)]
    for copy in copies:
        copy.start()
    for copy in copies:
        copy.wait()


def local(queries, keys, values, out_weight, out_grad, block_doc):
    seq_count, head_count = lax.axis_size("seq"), lax.axis_size("head")
    _, leaf, feats = queries.shape
    model = out_weight.shape[1]
    _, _, cols = pieces_of(seq_count, leaf)
    half = cols // 2
    heads = feats // DH
    gcols = GROUP_HEADS * DH
    groups = feats // gcols
    kcols = model // seq_count
    levels = seq_count.bit_length() - 1
    dma = pltpu.SemaphoreType.DMA
    vmem = pl.BlockSpec(memory_space=pltpu.VMEM)
    block = jax.ShapeDtypeStruct((leaf, feats), BF16)
    results = pl.pallas_call(
        functools.partial(kernel, seq_count, head_count, leaf, feats),
        out_shape=[block] * 4 + [jax.ShapeDtypeStruct((feats, kcols), BF16)],
        in_specs=[pl.BlockSpec(memory_space=pltpu.SMEM)] + [vmem] * 4
        + [pl.BlockSpec(memory_space=pl.ANY)],
        out_specs=[vmem] * 5,
        scratch_shapes=[
            pltpu.VMEM((head_count, feats, feats), BF16),
            pltpu.VMEM((head_count, leaf, feats), BF16),
            pltpu.VMEM((2, cols, feats), BF16),
            pltpu.VMEM((2, half - leaf, feats), BF16),
            pltpu.VMEM((heads, cols, leaf), BF16),
            pltpu.VMEM((seq_count, feats, leaf), BF16),
            pltpu.VMEM((seq_count, leaf, kcols), BF16),
            pltpu.VMEM((feats, leaf), F32),
            pltpu.VMEM((feats, leaf), BF16),
            pltpu.VMEM((groups, 2, leaf, gcols), F32),
            pltpu.VMEM((groups, 2, cols, gcols), BF16),
            pltpu.VMEM((groups, 2, half, gcols), BF16),
            pltpu.VMEM((groups, levels - 1, 2, leaf // 2, gcols), BF16),
            pltpu.VMEM((feats, kcols), F32),
            dma((head_count,)), dma((head_count,)), dma((head_count,)), dma((head_count,)),
            dma((seq_count,)), dma((seq_count,)), dma((seq_count,)), dma((seq_count,)),
            dma((seq_count, 2)), dma((seq_count, 2)), dma((groups,)), dma((groups,)),
            dma((groups, levels - 1)), dma((groups, levels - 1)),
        ],
        compiler_params=pltpu.CompilerParams(
            collective_id=0, has_side_effects=True, vmem_limit_bytes=60 * 1024 * 1024),
        cost_estimate=pl.CostEstimate(
            flops=8 * 10**9, bytes_accessed=16 * 2**20, transcendentals=2 * 2**20),
        name="hier_attention",
    )(block_doc, queries[0], keys[0], values[0], out_grad[0], out_weight)
    anywhere = pl.BlockSpec(memory_space=pl.ANY)
    context, query_grad, key_grad, value_grad, weight_grad = pl.pallas_call(
        copy_kernel,
        out_shape=[jax.ShapeDtypeStruct(r.shape, r.dtype) for r in results],
        in_specs=[anywhere] * 5,
        out_specs=[anywhere] * 5,
        scratch_shapes=[dma((5,))],
        compiler_params=pltpu.CompilerParams(vmem_limit_bytes=60 * 1024 * 1024),
        name="hand_over",
    )(*results)
    return context[None], query_grad[None], key_grad[None], value_grad[None], weight_grad


def solution(mesh):
    blocks = P(None, "seq", "head")
    return jax.shard_map(
        local,
        mesh=mesh,
        in_specs=(blocks, blocks, blocks, P("head", None), blocks, P()),
        out_specs=(blocks, blocks, blocks, blocks, P("head", "seq")),
        check_vma=False,
    )
```

```python
import functools
import math

import jax
import jax.numpy as jnp
from jax import lax
from jax.experimental import pallas as pl
from jax.experimental.pallas import tpu as pltpu
from jax.sharding import PartitionSpec as P

DH = 128
GROUP_HEADS = 2
F32 = jnp.float32
BF16 = jnp.bfloat16


def flipped(index, mask):
    out = index
    bit = 1
    while bit <= mask:
        if mask & bit:
            out = out + (1 - 2 * lax.rem(lax.div(index, jnp.int32(bit)), jnp.int32(2))) * bit
        bit *= 2
    return out


def top_bit(o):
    return 1 << (o.bit_length() - 1)


def dot_nn(a, b):
    return lax.dot_general(a, b, (((1,), (0,)), ((), ())), preferred_element_type=F32)


def dot_nt(a, b):
    return lax.dot_general(a, b, (((1,), (1,)), ((), ())), preferred_element_type=F32)


def dot_tn(a, b):
    return lax.dot_general(a, b, (((0,), (0,)), ((), ())), preferred_element_type=F32)


def pieces_of(seq_count, leaf):
    rows, starts, at = {}, {}, 0
    for parity in (0, 1):
        for o in range(parity, seq_count, 2):
            level = max(o.bit_length() - 1, 0)
            rows[o], starts[o] = leaf >> level, at
            at += rows[o]
    return rows, starts, at


def kernel(seq_count, head_count, leaf, feats,
           doc, q_ref, k_ref, v_ref, og_ref, w_ref,
           ctx_out, dq_out, dk_out, dv_out, wg_out,
           wv, ogf, kc, pb, probs, ctxs, ogs, cga, cgt, own, dbuf, pair, back, acc,
           s_w, s_up, s_dn, r_z, s_kv, r_kv, s_a, r_a, s_c, r_c, s_p, r_p, s_g, r_g):
    me = lax.axis_index("seq")
    z = lax.axis_index("head")
    partner = flipped(me, 1)
    levels = seq_count.bit_length() - 1
    rows, starts, cols = pieces_of(seq_count, leaf)
    half = cols // 2
    heads = feats // DH
    gcols = GROUP_HEADS * DH
    groups = feats // gcols
    per_shard = seq_count // head_count
    kcols = feats // per_shard
    hf = feats // 2
    scaling = 1.0 / math.sqrt(DH)

    def remote(src, dst, send, recv, **where):
        return pltpu.make_async_remote_copy(
            src_ref=src, dst_ref=dst, send_sem=send, recv_sem=recv,
            device_id=where, device_id_type=pl.DeviceIdType.MESH)

    def arrived(dst, recv):
        remote(dst, dst, recv, recv, seq=partner).wait_recv()

    def w_copy(zp):
        return pltpu.make_async_copy(
            w_ref.at[:, pl.ds(zp * feats, feats)], wv.at[zp], s_w.at[zp])

    def z_copy(zp, step, sem):
        sems = s_up if step > 0 else s_dn
        return remote(ogf.at[zp], ogf.at[zp], sems.at[sem], r_z.at[zp], head=z + step)

    def own_sends(act):
        for step in (1, 2):
            @pl.when(z + step < head_count)
            def _():
                act(z_copy(z, step, head_count + step - 1))

            @pl.when(z >= step)
            def _():
                act(z_copy(z, -step, head_count + step - 1))

    def kv_slot(o, n):
        return kc.at[:, pl.ds(starts[o], rows[o]), pl.ds(n * hf, hf)]

    def kv_copy(o, n):
        if o == 0:
            src, dst, to = kv_slot(0, n), 1, partner
        elif o % 2 == 0:
            src = pb.at[:, pl.ds(starts[o] - leaf, rows[o]), pl.ds(n * hf, hf)]
            dst, to = o, flipped(me, top_bit(o))
        else:
            src, dst, to = kv_slot(o - 1, n), o, partner
        return remote(src, kv_slot(dst, n), s_kv.at[o, n], r_kv.at[dst, n], seq=to)

    def kv_arrived(o, n):
        arrived(kv_slot(o, n), r_kv.at[o, n])

    def a_copy(zp, j):
        to = zp * per_shard + j
        return remote(ogf.at[zp, :, pl.ds(j * kcols, kcols)], ogs.at[me],
                      s_a.at[to], r_a.at[me], seq=to)

    def c_copy(o, n):
        if o == top_bit(o):
            src, bit = 0, o
        elif o % 2 == 1:
            src, bit = o - 1, 1
        else:
            bit = o & -o if n else top_bit(o)
            src = o ^ bit
        part = pl.ds(n * hf, hf)
        return remote(ctxs.at[src, part], ctxs.at[o, part], s_c.at[o, n], r_c.at[o, n],
                      seq=flipped(me, bit))

    def c_pass(o, n):
        c_copy(o, n).wait_recv()
        c_copy(o + 1, n).start()
        for level in range(1, levels):
            bit = 1 << level
            to = o | bit
            if not o & bit and bit == (to & -to if n else top_bit(to)):
                c_copy(to, n).start()

    def p_copy(g):
        return remote(dbuf.at[g, :, pl.ds(half, half)], pair.at[g], s_p.at[g], r_p.at[g],
                      seq=partner)

    def level_rows(level):
        return starts[1 << level], (leaf >> level) << (level - 1)

    def g_copy(g, level):
        at, n = level_rows(level)
        return remote(dbuf.at[g, :, pl.ds(at, n)], back.at[g, level - 1],
                      s_g.at[g, level - 1], r_g.at[g, level - 1], seq=flipped(me, 1 << level))

    far = list(range(2, seq_count, 2))

    for zp in range(head_count):
        w_copy(zp).start()
    barrier = pltpu.get_barrier_semaphore()
    for o in range(1, seq_count):
        pl.semaphore_signal(barrier, inc=1, device_id={"seq": flipped(me, o)},
                            device_id_type=pl.DeviceIdType.MESH)

    for step in range(1, head_count):
        pl.semaphore_signal(barrier, inc=1, device_id={"head": lax.rem(z + step, head_count)},
                            device_id_type=pl.DeviceIdType.MESH)

    ogf[z] = og_ref[...]
    kc[0, 0:leaf] = k_ref[...]
    kc[1, 0:leaf] = v_ref[...]

    def pool_from(source, low, r, n_half):
        for which in range(2):
            for c in range(n_half * hf, n_half * hf + hf, 256):
                piece = source(which, c)
                for level in range(low + 1, levels):
                    n = leaf >> level
                    pool = jnp.where(
                        lax.shift_right_logical(
                            lax.broadcasted_iota(jnp.int32, (n, 2 * n), 1), 1)
                        == lax.broadcasted_iota(jnp.int32, (n, 2 * n), 0), 0.5, 0.0).astype(BF16)
                    piece = dot_nn(pool, piece).astype(BF16)
                    at = starts[(1 << level) + r] - leaf
                    pb[which, at:at + n, c:c + 256] = piece

    for n in range(2):
        pool_from(lambda which, c: (k_ref, v_ref)[which][:, c:c + 256], 0, 0, n)
    pl.semaphore_wait(barrier, seq_count - 1 + head_count - 1)

    own_sends(lambda copy: copy.start())
    for n in range(2):
        for level in range(1, levels):
            kv_copy(1 << level, n).start()
        kv_copy(0, n).start()

    def scatter_grad(zp):
        for j in range(per_shard):
            @pl.when(zp * per_shard + j != me)
            def _():
                a_copy(zp, j).start()

            @pl.when(zp * per_shard + j == me)
            def _():
                ogs[me] = ogf[zp, :, j * kcols:(j + 1) * kcols]

    def project(zp, first=False):
        grad = ogf[zp]

        @pl.loop(0, feats // 256)
        def _(t):
            at = pl.ds(pl.multiple_of(t * 256, 256), 256)
            term = dot_nt(wv[zp, at], grad)
            cga[at] = term if first else cga[at] + term

    def gather_step(k):
        @pl.when(z >= k)
        def _():
            zp = z - k
            arrived(ogf.at[zp], r_z.at[zp])
            if k >= 2:
                @pl.when(z < head_count - 1)
                def _():
                    z_copy(zp, 1, zp).start()

        @pl.when(z + k < head_count)
        def _():
            zp = z + k
            arrived(ogf.at[zp], r_z.at[zp])
            if k >= 2:
                @pl.when(z > 0)
                def _():
                    z_copy(zp, -1, zp).start()

        @pl.when(z >= k)
        def _():
            scatter_grad(z - k)
            project(z - k)

        @pl.when(z + k < head_count)
        def _():
            scatter_grad(z + k)
            project(z + k)

    def columns(n):
        for o in far:
            kv_arrived(o, n)
            kv_copy(o + 1, n).start()
            low = o.bit_length() - 1
            if low + 1 < levels:
                pool_from(
                    lambda which, c: kc[which, starts[o]:starts[o] + rows[o], c:c + 256],
                    low, o, n)
                for level in range(low + 1, levels):
                    kv_copy((1 << level) + o, n).start()
        kv_arrived(1, n)
        for o in far:
            kv_arrived(o + 1, n)

    for zp in range(head_count):
        w_copy(zp).wait()
    project(z, first=True)

    log2e = 1.4426950408889634
    my_doc = doc[0, me]
    biases = []
    for o in sorted(starts, key=lambda p: starts[p]):
        level = float(max(o.bit_length() - 1, 0))
        same = doc[0, flipped(me, o)] == my_doc
        biases.append((starts[o], rows[o], jnp.where(same, level, -1e30).astype(F32)))

    def forward(first, last):
        @pl.loop(first, last)
        def _(h):
            at = pl.ds(pl.multiple_of(h * DH, DH), DH)
            keys, vals, query = kc[0, :, at], kc[1, :, at], q_ref[:, at]
            raw = dot_nt(keys, query)
            shifted = jnp.concatenate(
                [raw[s:s + n] * (scaling * log2e) + b for s, n, b in biases], axis=0)
            top = jnp.max(shifted, axis=0, keepdims=True)
            weights = jnp.exp2(shifted - top)
            inv = 1.0 / jnp.sum(weights, axis=0, keepdims=True)
            prob = (weights * inv).astype(BF16)
            probs[h] = prob
            out = dot_tn(vals, prob)
            ctxs[0, at] = out.astype(BF16)
            ctx_out[:, at] = out.T.astype(BF16)

    def send_context(n):
        for level in range(levels - 1, -1, -1):
            c_copy(1 << level, n).start()

    columns(0)
    forward(0, heads // 2)
    send_context(0)
    columns(1)
    scatter_grad(z)
    forward(heads // 2, heads)
    send_context(1)
    gather_step(1)
    for k in range(2, head_count - 1):
        gather_step(k)
    for o in far:
        c_pass(o, 0)
    gather_step(head_count - 1)
    cgt[...] = cga[...].astype(BF16)

    def spread_from(level):
        at, n = level_rows(level)
        row = lax.broadcasted_iota(jnp.int32, (at, n), 0)
        col = lax.broadcasted_iota(jnp.int32, (at, n), 1)
        out = jnp.zeros((at, n), F32)
        for r in range(0, 1 << level, 2):
            low = max(r.bit_length() - 1, 0)
            first = starts[(1 << level) + r] - at
            inside = (row >= starts[r]) & (row < starts[r] + rows[r])
            hit = lax.shift_right_logical(row - starts[r], level - low) == col - first
            out = jnp.where(inside & hit, 0.5 ** (level - low), out)
        return out.astype(BF16)

    def finish_pair(g):
        arrived(pair.at[g], r_p.at[g])
        for which in range(2):
            own[g, which] += pair[g, which, :leaf].astype(F32)
            dbuf[g, which, leaf:half] = (
                dbuf[g, which, leaf:half].astype(F32) + pair[g, which, leaf:half].astype(F32)
            ).astype(BF16)
        g_copy(g, levels - 1).start()

    def finish_level(g, level, spread):
        at, n = level_rows(level)
        arrived(back.at[g, level - 1], r_g.at[g, level - 1])
        for which in range(2):
            more = dot_nn(spread, back[g, level - 1, which])
            own[g, which] += more[:leaf]
            if at > leaf:
                dbuf[g, which, leaf:at] = (
                    dbuf[g, which, leaf:at].astype(F32) + more[leaf:]).astype(BF16)
        if level > 1:
            g_copy(g, level - 1).start()

    top_spread = spread_from(levels - 1)

    def add_weight(o, first=False):
        src = flipped(me, o)
        if o:
            arrived(ogs.at[src], r_a.at[src])
        grad = ogs[src]

        @pl.loop(0, feats // 256)
        def _(t):
            at = pl.ds(pl.multiple_of(t * 256, 256), 256)
            term = dot_nn(ctxs[o, at], grad)
            acc[at] = term if first else acc[at] + term

    @pl.loop(0, groups)
    def _(g):
        for i in range(GROUP_HEADS):
            h = g * GROUP_HEADS + i
            at = pl.ds(pl.multiple_of(h * DH, DH), DH)
            lanes = slice(i * DH, (i + 1) * DH)
            keys, vals, query = kc[0, :, at], kc[1, :, at], q_ref[:, at]
            grad = cgt[at]
            prob = probs[h]
            delta = jnp.sum(grad.astype(F32) * ctxs[0, at].astype(F32), axis=0, keepdims=True)
            prob_grad = dot_nn(vals, grad)
            score_grad = (prob.astype(F32) * (prob_grad - delta)).astype(BF16)
            dq_out[:, at] = (dot_tn(keys, score_grad) * scaling).T.astype(BF16)
            dk = dot_nn(score_grad, query) * scaling
            dv = dot_nt(prob, grad)
            for which, full in enumerate((dk, dv)):
                own[g, which, :, lanes] = full[:leaf]
                dbuf[g, which, leaf:, lanes] = full[leaf:].astype(BF16)
        p_copy(g).start()

        @pl.when(g > 0)
        def _():
            finish_pair(g - 1)

        if levels > 2:
            @pl.when(g > 1)
            def _():
                finish_level(g - 2, levels - 1, top_spread)

        @pl.when(g == groups // 2)
        def _():
            for level in range(1, levels):
                c_pass(1 << level, 1)

    finish_pair(groups - 1)
    for o in far:
        if o != top_bit(o):
            c_pass(o, 1)
    add_weight(0, first=True)
    for level in range(levels - 1, 1, -1):
        spread = spread_from(level)

        @pl.loop(max(groups - 2, 0) if level == levels - 1 else 0, groups)
        def _(g):
            finish_level(g, level, spread)

    for n in range(2):
        c_copy(1, n).wait_recv()
    add_weight(1)
    for o in far:
        add_weight(o)
    for o in far:
        for n in range(2):
            c_copy(o + 1, n).wait_recv()
        add_weight(o + 1)

    wg_out[...] = acc[...].astype(BF16)

    last = spread_from(1)
    for g in range(groups):
        finish_level(g, 1, last)
        for which, out in enumerate((dk_out, dv_out)):
            out[:, g * gcols:(g + 1) * gcols] = own[g, which].astype(BF16)

    own_sends(lambda copy: copy.wait_send())
    for zp in range(head_count):
        @pl.when((z < head_count - 1) & (z - zp >= 2))
        def _():
            z_copy(zp, 1, zp).wait_send()

        @pl.when((z > 0) & (zp - z >= 2))
        def _():
            z_copy(zp, -1, zp).wait_send()

        for j in range(per_shard):
            @pl.when(zp * per_shard + j != me)
            def _():
                a_copy(zp, j).wait_send()
    for n in range(2):
        kv_copy(0, n).wait_send()
        for o in far:
            kv_copy(o, n).wait_send()
            kv_copy(o + 1, n).wait_send()
        for o in range(1, seq_count):
            c_copy(o, n).wait_send()
    for g in range(groups):
        p_copy(g).wait_send()
        for level in range(1, levels):
            g_copy(g, level).wait_send()


def copy_kernel(*refs):
    count = len(refs) // 2
    for i in range(count):
        refs[count + i][...] = refs[i][...]


def local(queries, keys, values, out_weight, out_grad, block_doc):
    seq_count, head_count = lax.axis_size("seq"), lax.axis_size("head")
    _, leaf, feats = queries.shape
    model = out_weight.shape[1]
    _, _, cols = pieces_of(seq_count, leaf)
    half = cols // 2
    heads = feats // DH
    gcols = GROUP_HEADS * DH
    groups = feats // gcols
    kcols = model // seq_count
    levels = seq_count.bit_length() - 1
    dma = pltpu.SemaphoreType.DMA
    vmem = pl.BlockSpec(memory_space=pltpu.VMEM)
    block = jax.ShapeDtypeStruct((leaf, feats), BF16)
    results = pl.pallas_call(
        functools.partial(kernel, seq_count, head_count, leaf, feats),
        out_shape=[block] * 4 + [jax.ShapeDtypeStruct((feats, kcols), BF16)],
        in_specs=[pl.BlockSpec(memory_space=pltpu.SMEM)] + [vmem] * 4
        + [pl.BlockSpec(memory_space=pl.ANY)],
        out_specs=[vmem] * 5,
        scratch_shapes=[
            pltpu.VMEM((head_count, feats, feats), BF16),
            pltpu.VMEM((head_count, leaf, feats), BF16),
            pltpu.VMEM((2, cols, feats), BF16),
            pltpu.VMEM((2, half - leaf, feats), BF16),
            pltpu.VMEM((heads, cols, leaf), BF16),
            pltpu.VMEM((seq_count, feats, leaf), BF16),
            pltpu.VMEM((seq_count, leaf, kcols), BF16),
            pltpu.VMEM((feats, leaf), F32),
            pltpu.VMEM((feats, leaf), BF16),
            pltpu.VMEM((groups, 2, leaf, gcols), F32),
            pltpu.VMEM((groups, 2, cols, gcols), BF16),
            pltpu.VMEM((groups, 2, half, gcols), BF16),
            pltpu.VMEM((groups, levels - 1, 2, leaf // 2, gcols), BF16),
            pltpu.VMEM((feats, kcols), F32),
            dma((head_count,)), dma((head_count + 2,)), dma((head_count + 2,)),
            dma((head_count,)), dma((seq_count, 2)), dma((seq_count, 2)),
            dma((seq_count,)), dma((seq_count,)),
            dma((seq_count, 2)), dma((seq_count, 2)), dma((groups,)), dma((groups,)),
            dma((groups, levels - 1)), dma((groups, levels - 1)),
        ],
        compiler_params=pltpu.CompilerParams(
            collective_id=0, has_side_effects=True, vmem_limit_bytes=60 * 1024 * 1024),
        cost_estimate=pl.CostEstimate(
            flops=8 * 10**9, bytes_accessed=16 * 2**20, transcendentals=2 * 2**20),
        name="hier_attention",
    )(block_doc, queries[0], keys[0], values[0], out_grad[0], out_weight)
    steps = 4
    tiles = [pl.BlockSpec((r.shape[0] // steps, r.shape[1]), lambda i: (i, 0)) for r in results]
    context, query_grad, key_grad, value_grad, weight_grad = pl.pallas_call(
        copy_kernel,
        grid=(steps,),
        out_shape=[jax.ShapeDtypeStruct(r.shape, r.dtype) for r in results],
        in_specs=tiles,
        out_specs=tiles,
        compiler_params=pltpu.CompilerParams(vmem_limit_bytes=60 * 1024 * 1024),
        name="hand_over",
    )(*results)
    return context[None], query_grad[None], key_grad[None], value_grad[None], weight_grad


def solution(mesh):
    blocks = P(None, "seq", "head")
    return jax.shard_map(
        local,
        mesh=mesh,
        in_specs=(blocks, blocks, blocks, P("head", None), blocks, P()),
        out_specs=(blocks, blocks, blocks, blocks, P("head", "seq")),
        check_vma=False,
    )
```

```python
import functools
import math

import jax
import jax.numpy as jnp
from jax import lax
from jax.experimental import pallas as pl
from jax.experimental.pallas import tpu as pltpu
from jax.sharding import PartitionSpec as P

DH = 128
GROUP_HEADS = 2
F32 = jnp.float32
BF16 = jnp.bfloat16


def flipped(index, mask):
    out = index
    bit = 1
    while bit <= mask:
        if mask & bit:
            out = out + (1 - 2 * lax.rem(lax.div(index, jnp.int32(bit)), jnp.int32(2))) * bit
        bit *= 2
    return out


def dot_nn(a, b):
    return lax.dot_general(a, b, (((1,), (0,)), ((), ())), preferred_element_type=F32)


def dot_nt(a, b):
    return lax.dot_general(a, b, (((1,), (1,)), ((), ())), preferred_element_type=F32)


def dot_tn(a, b):
    return lax.dot_general(a, b, (((0,), (0,)), ((), ())), preferred_element_type=F32)


def pieces_of(seq_count, leaf):
    rows, starts, at = {}, {}, 0
    for parity in (0, 1):
        for o in range(parity, seq_count, 2):
            level = max(o.bit_length() - 1, 0)
            rows[o], starts[o] = leaf >> level, at
            at += rows[o]
    return rows, starts, at


def kernel(seq_count, head_count, leaf, feats,
           doc, q_ref, k_ref, v_ref, og_ref, w_ref,
           ctx_out, dq_out, dk_out, dv_out, wg_out,
           wv, ogf, kc, pb, probs, ctxs, ogs, cga, cgt, own, dbuf, pair, back, acc,
           s_w, s_up, s_dn, r_z, s_kv, r_kv, s_a, r_a, s_c, r_c, s_p, r_p, s_g, r_g):
    me = lax.axis_index("seq")
    z = lax.axis_index("head")
    partner = flipped(me, 1)
    levels = seq_count.bit_length() - 1
    rows, starts, cols = pieces_of(seq_count, leaf)
    half = cols // 2
    heads = feats // DH
    gcols = GROUP_HEADS * DH
    groups = feats // gcols
    per_shard = seq_count // head_count
    kcols = feats // per_shard
    scaling = 1.0 / math.sqrt(DH)

    def remote(src, dst, send, recv, **where):
        return pltpu.make_async_remote_copy(
            src_ref=src, dst_ref=dst, send_sem=send, recv_sem=recv,
            device_id=where, device_id_type=pl.DeviceIdType.MESH)

    def arrived(dst, recv):
        remote(dst, dst, recv, recv, seq=partner).wait_recv()

    def w_copy(zp):
        return pltpu.make_async_copy(
            w_ref.at[:, pl.ds(zp * feats, feats)], wv.at[zp], s_w.at[zp])

    def up_copy(zp):
        return remote(ogf.at[zp], ogf.at[zp], s_up.at[zp], r_z.at[zp], head=z + 1)

    def down_copy(zp):
        return remote(ogf.at[zp], ogf.at[zp], s_dn.at[zp], r_z.at[zp], head=z - 1)

    def kv_copy(o):
        if o == 0:
            src, dst, to = kc.at[:, pl.ds(0, leaf)], 1, partner
        elif o % 2 == 0:
            level = o.bit_length() - 1
            src = pb.at[:, pl.ds(leaf - (leaf >> (level - 1)), rows[o])]
            dst, to = o, flipped(me, o)
        else:
            src, dst, to = kc.at[:, pl.ds(starts[o - 1], rows[o])], o, partner
        slot = kc.at[:, pl.ds(starts[dst], rows[dst])]
        return remote(src, slot, s_kv.at[o], r_kv.at[dst], seq=to)

    def kv_arrived(o):
        arrived(kc.at[:, pl.ds(starts[o], rows[o])], r_kv.at[o])

    def a_copy(zp, j):
        to = zp * per_shard + j
        return remote(ogf.at[zp, :, pl.ds(j * kcols, kcols)], ogs.at[me],
                      s_a.at[to], r_a.at[me], seq=to)

    def c_copy(o, n):
        part = pl.ds(n * (feats // 2), feats // 2)
        src, to = (0, flipped(me, o)) if o == 1 or o % 2 == 0 else (o - 1, partner)
        return remote(ctxs.at[src, part], ctxs.at[o, part], s_c.at[o, n], r_c.at[o, n], seq=to)

    def p_copy(g):
        return remote(dbuf.at[g, :, pl.ds(half, half)], pair.at[g], s_p.at[g], r_p.at[g],
                      seq=partner)

    def g_copy(g, o):
        return remote(dbuf.at[g, :, pl.ds(starts[o], rows[o])],
                      back.at[g, :, pl.ds(starts[o] - leaf, rows[o])],
                      s_g.at[g, o // 2], r_g.at[g, o // 2], seq=flipped(me, o))

    far = list(range(2, seq_count, 2))

    for zp in range(head_count):
        w_copy(zp).start()
    barrier = pltpu.get_barrier_semaphore()
    for o in range(1, seq_count):
        pl.semaphore_signal(barrier, inc=1, device_id={"seq": flipped(me, o)},
                            device_id_type=pl.DeviceIdType.MESH)

    @pl.when(z > 0)
    def _():
        pl.semaphore_signal(barrier, inc=1, device_id={"head": z - 1},
                            device_id_type=pl.DeviceIdType.MESH)

    @pl.when(z < head_count - 1)
    def _():
        pl.semaphore_signal(barrier, inc=1, device_id={"head": z + 1},
                            device_id_type=pl.DeviceIdType.MESH)

    ogf[z] = og_ref[...]
    kc[0, 0:leaf] = k_ref[...]
    kc[1, 0:leaf] = v_ref[...]
    for which, ref in enumerate((k_ref, v_ref)):
        for c in range(0, feats, 256):
            block = ref[:, c:c + 256]
            at = 0
            for level in range(1, levels):
                n = leaf >> level
                pool = jnp.where(
                    lax.broadcasted_iota(jnp.int32, (n, 2 * n), 1) // 2
                    == lax.broadcasted_iota(jnp.int32, (n, 2 * n), 0), 0.5, 0.0).astype(BF16)
                block = dot_nn(pool, block).astype(BF16)
                pb[which, at:at + n, c:c + 256] = block
                at += n
    inner = (z > 0) & (z < head_count - 1)

    @pl.when(inner)
    def _():
        pl.semaphore_wait(barrier, seq_count + 1)

    @pl.when(jnp.logical_not(inner))
    def _():
        pl.semaphore_wait(barrier, seq_count)

    @pl.when(z > 0)
    def _():
        down_copy(z).start()

    @pl.when(z < head_count - 1)
    def _():
        up_copy(z).start()

    kv_copy(0).start()
    for o in far:
        kv_copy(o).start()

    def scatter_grad(zp):
        for j in range(per_shard):
            @pl.when(zp * per_shard + j != me)
            def _():
                a_copy(zp, j).start()

            @pl.when(zp * per_shard + j == me)
            def _():
                ogs[me] = ogf[zp, :, j * kcols:(j + 1) * kcols]

    def project(zp, first=False):
        grad = ogf[zp]

        @pl.loop(0, feats // 256)
        def _(t):
            at = pl.ds(pl.multiple_of(t * 256, 256), 256)
            term = dot_nt(wv[zp, at], grad)
            cga[at] = term if first else cga[at] + term

    def gather_step(k):
        @pl.when(z >= k)
        def _():
            zp = z - k
            arrived(ogf.at[zp], r_z.at[zp])

            @pl.when(z < head_count - 1)
            def _():
                up_copy(zp).start()

        @pl.when(z + k < head_count)
        def _():
            zp = z + k
            arrived(ogf.at[zp], r_z.at[zp])

            @pl.when(z > 0)
            def _():
                down_copy(zp).start()

        @pl.when(z >= k)
        def _():
            if k > 1:
                scatter_grad(z - k)
            project(z - k)

        @pl.when(z + k < head_count)
        def _():
            if k > 1:
                scatter_grad(z + k)
            project(z + k)

    for zp in range(head_count):
        w_copy(zp).wait()
    project(z, first=True)
    gather_step(1)

    for o in far:
        kv_arrived(o)
        kv_copy(o + 1).start()
    kv_arrived(1)
    for o in far:
        kv_arrived(o + 1)
    scatter_grad(z)

    @pl.when(z >= 1)
    def _():
        scatter_grad(z - 1)

    @pl.when(z + 1 < head_count)
    def _():
        scatter_grad(z + 1)

    log2e = 1.4426950408889634
    my_doc = doc[0, me]
    biases = []
    for o in sorted(starts, key=lambda p: starts[p]):
        level = float(max(o.bit_length() - 1, 0))
        same = doc[0, flipped(me, o)] == my_doc
        biases.append((starts[o], rows[o], jnp.where(same, level, -1e30).astype(F32)))

    def forward(first, last):
        @pl.loop(first, last)
        def _(h):
            at = pl.ds(pl.multiple_of(h * DH, DH), DH)
            keys, vals, query = kc[0, :, at], kc[1, :, at], q_ref[:, at]
            raw = dot_nt(keys, query)
            shifted = jnp.concatenate(
                [raw[s:s + n] * (scaling * log2e) + b for s, n, b in biases], axis=0)
            top = jnp.max(shifted, axis=0, keepdims=True)
            weights = jnp.exp2(shifted - top)
            inv = 1.0 / jnp.sum(weights, axis=0, keepdims=True)
            prob = (weights * inv).astype(BF16)
            probs[h] = prob
            out = dot_tn(vals, prob)
            ctxs[0, at] = out.astype(BF16)
            ctx_out[:, at] = out.T.astype(BF16)

    forward(0, heads // 2)
    for o in far + [1]:
        c_copy(o, 0).start()
    if head_count > 2:
        gather_step(2)
    forward(heads // 2, heads)
    for o in far + [1]:
        c_copy(o, 1).start()
    for k in range(3, head_count):
        gather_step(k)
    cgt[...] = cga[...].astype(BF16)

    def finish(g):
        arrived(pair.at[g], r_p.at[g])
        for which in range(2):
            dbuf[g, which, leaf:half] = (
                dbuf[g, which, leaf:half].astype(F32) + pair[g, which, leaf:half].astype(F32)
            ).astype(BF16)
        for o in far:
            g_copy(g, o).start()

    @pl.loop(0, groups)
    def _(g):
        for i in range(GROUP_HEADS):
            h = g * GROUP_HEADS + i
            at = pl.ds(pl.multiple_of(h * DH, DH), DH)
            lanes = slice(i * DH, (i + 1) * DH)
            keys, vals, query = kc[0, :, at], kc[1, :, at], q_ref[:, at]
            grad = cgt[at]
            prob = probs[h]
            delta = jnp.sum(grad.astype(F32) * ctxs[0, at].astype(F32), axis=0, keepdims=True)
            prob_grad = dot_nn(vals, grad)
            score_grad = (prob.astype(F32) * (prob_grad - delta)).astype(BF16)
            dq_out[:, at] = (dot_tn(keys, score_grad) * scaling).T.astype(BF16)
            dk = dot_nn(score_grad, query) * scaling
            dv = dot_nt(prob, grad)
            for which, full in enumerate((dk, dv)):
                own[g, which, :, lanes] = full[:leaf]
                dbuf[g, which, leaf:, lanes] = full[leaf:].astype(BF16)
        p_copy(g).start()

        @pl.when(g > 0)
        def _():
            finish(g - 1)

    finish(groups - 1)

    for o in far:
        for n in range(2):
            c_copy(o, n).wait_recv()
            c_copy(o + 1, n).start()
    for n, o in enumerate([0, 1] + far + [o + 1 for o in far]):
        if o % 2 == 1:
            for n in range(2):
                c_copy(o, n).wait_recv()
        src = flipped(me, o)
        if o:
            arrived(ogs.at[src], r_a.at[src])
        grad = ogs[src]

        @pl.loop(0, feats // 256)
        def _(t):
            at = pl.ds(pl.multiple_of(t * 256, 256), 256)
            term = dot_nn(ctxs[o, at], grad)
            acc[at] = term if n == 0 else acc[at] + term

    wg_out[...] = acc[...].astype(BF16)

    far_rows = half - leaf
    r_id = lax.broadcasted_iota(jnp.int32, (leaf, far_rows), 0)
    c_id = lax.broadcasted_iota(jnp.int32, (leaf, far_rows), 1)
    spread = jnp.zeros((leaf, far_rows), F32)
    for o in far:
        level = o.bit_length() - 1
        hit = (lax.shift_right_logical(r_id, level) == c_id - (starts[o] - leaf))
        spread = jnp.where(hit, 0.5 ** level, spread)
    spread = spread.astype(BF16)
    for g in range(groups):
        for o in far:
            arrived(back.at[g, :, pl.ds(starts[o] - leaf, rows[o])], r_g.at[g, o // 2])
        for which, out in enumerate((dk_out, dv_out)):
            total = own[g, which] + pair[g, which, :leaf].astype(F32) + dot_nn(
                spread, back[g, which])
            out[:, g * gcols:(g + 1) * gcols] = total.astype(BF16)

    for zp in range(head_count):
        @pl.when((z < head_count - 1) & (zp <= z))
        def _():
            up_copy(zp).wait_send()

        @pl.when((z > 0) & (zp >= z))
        def _():
            down_copy(zp).wait_send()

        for j in range(per_shard):
            @pl.when(zp * per_shard + j != me)
            def _():
                a_copy(zp, j).wait_send()
    kv_copy(0).wait_send()
    for o in far:
        kv_copy(o).wait_send()
        kv_copy(o + 1).wait_send()
    for o in range(1, seq_count):
        for n in range(2):
            c_copy(o, n).wait_send()
    for g in range(groups):
        p_copy(g).wait_send()
        for o in far:
            g_copy(g, o).wait_send()


def copy_kernel(*refs):
    count = len(refs) // 2
    for i in range(count):
        refs[count + i][...] = refs[i][...]


def local(queries, keys, values, out_weight, out_grad, block_doc):
    seq_count, head_count = lax.axis_size("seq"), lax.axis_size("head")
    _, leaf, feats = queries.shape
    model = out_weight.shape[1]
    _, _, cols = pieces_of(seq_count, leaf)
    half = cols // 2
    heads = feats // DH
    gcols = GROUP_HEADS * DH
    groups = feats // gcols
    kcols = model // seq_count
    dma = pltpu.SemaphoreType.DMA
    vmem = pl.BlockSpec(memory_space=pltpu.VMEM)
    block = jax.ShapeDtypeStruct((leaf, feats), BF16)
    results = pl.pallas_call(
        functools.partial(kernel, seq_count, head_count, leaf, feats),
        out_shape=[block] * 4 + [jax.ShapeDtypeStruct((feats, kcols), BF16)],
        in_specs=[pl.BlockSpec(memory_space=pltpu.SMEM)] + [vmem] * 4
        + [pl.BlockSpec(memory_space=pl.ANY)],
        out_specs=[vmem] * 5,
        scratch_shapes=[
            pltpu.VMEM((head_count, feats, feats), BF16),
            pltpu.VMEM((head_count, leaf, feats), BF16),
            pltpu.VMEM((2, cols, feats), BF16),
            pltpu.VMEM((2, leaf, feats), BF16),
            pltpu.VMEM((heads, cols, leaf), BF16),
            pltpu.VMEM((seq_count, feats, leaf), BF16),
            pltpu.VMEM((seq_count, leaf, kcols), BF16),
            pltpu.VMEM((feats, leaf), F32),
            pltpu.VMEM((feats, leaf), BF16),
            pltpu.VMEM((groups, 2, leaf, gcols), F32),
            pltpu.VMEM((groups, 2, cols, gcols), BF16),
            pltpu.VMEM((groups, 2, half, gcols), BF16),
            pltpu.VMEM((groups, 2, half - leaf, gcols), BF16),
            pltpu.VMEM((feats, kcols), F32),
            dma((head_count,)), dma((head_count,)), dma((head_count,)), dma((head_count,)),
            dma((seq_count,)), dma((seq_count,)), dma((seq_count,)), dma((seq_count,)),
            dma((seq_count, 2)), dma((seq_count, 2)), dma((groups,)), dma((groups,)),
            dma((groups, seq_count // 2)), dma((groups, seq_count // 2)),
        ],
        compiler_params=pltpu.CompilerParams(
            collective_id=0, has_side_effects=True, vmem_limit_bytes=60 * 1024 * 1024),
        cost_estimate=pl.CostEstimate(
            flops=8 * 10**9, bytes_accessed=16 * 2**20, transcendentals=2 * 2**20),
        name="hier_attention",
    )(block_doc, queries[0], keys[0], values[0], out_grad[0], out_weight)
    steps = 4
    tiles = [pl.BlockSpec((r.shape[0] // steps, r.shape[1]), lambda i: (i, 0)) for r in results]
    context, query_grad, key_grad, value_grad, weight_grad = pl.pallas_call(
        copy_kernel,
        grid=(steps,),
        out_shape=[jax.ShapeDtypeStruct(r.shape, r.dtype) for r in results],
        in_specs=tiles,
        out_specs=tiles,
        compiler_params=pltpu.CompilerParams(vmem_limit_bytes=60 * 1024 * 1024),
        name="hand_over",
    )(*results)
    return context[None], query_grad[None], key_grad[None], value_grad[None], weight_grad


def solution(mesh):
    blocks = P(None, "seq", "head")
    return jax.shard_map(
        local,
        mesh=mesh,
        in_specs=(blocks, blocks, blocks, P("head", None), blocks, P()),
        out_specs=(blocks, blocks, blocks, blocks, P("head", "seq")),
        check_vma=False,
    )
```

```python
import functools
import math

import jax
import jax.numpy as jnp
from jax import lax
from jax.experimental import pallas as pl
from jax.experimental.pallas import tpu as pltpu
from jax.sharding import PartitionSpec as P

DH = 128
GROUP_HEADS = 2
F32 = jnp.float32
BF16 = jnp.bfloat16


def flipped(index, mask):
    out = index
    bit = 1
    while bit <= mask:
        if mask & bit:
            out = out + (1 - 2 * lax.rem(lax.div(index, jnp.int32(bit)), jnp.int32(2))) * bit
        bit *= 2
    return out


def dot_nn(a, b):
    return lax.dot_general(a, b, (((1,), (0,)), ((), ())), preferred_element_type=F32)


def dot_nt(a, b):
    return lax.dot_general(a, b, (((1,), (1,)), ((), ())), preferred_element_type=F32)


def dot_tn(a, b):
    return lax.dot_general(a, b, (((0,), (0,)), ((), ())), preferred_element_type=F32)


def pieces_of(seq_count, leaf):
    rows, starts, at = {}, {}, 0
    for parity in (0, 1):
        for o in range(parity, seq_count, 2):
            level = max(o.bit_length() - 1, 0)
            rows[o], starts[o] = leaf >> level, at
            at += rows[o]
    return rows, starts, at


def kernel(seq_count, head_count, leaf, feats,
           doc, q_ref, k_ref, v_ref, og_ref, w_ref,
           ctx_out, dq_out, dk_out, dv_out, wg_out,
           wv, ogf, kc, pb, probs, ctxs, ogs, cga, cgt, own, dbuf, pair, back, acc,
           s_w, s_up, s_dn, r_z, s_kv, r_kv, s_a, r_a, s_c, r_c, s_p, r_p, s_g, r_g, sums, s_s, r_s):
    me = lax.axis_index("seq")
    z = lax.axis_index("head")
    partner = flipped(me, 1)
    levels = seq_count.bit_length() - 1
    rows, starts, cols = pieces_of(seq_count, leaf)
    half = cols // 2
    heads = feats // DH
    gcols = GROUP_HEADS * DH
    groups = feats // gcols
    per_shard = seq_count // head_count
    kcols = feats // per_shard
    scaling = 1.0 / math.sqrt(DH)

    def remote(src, dst, send, recv, **where):
        return pltpu.make_async_remote_copy(
            src_ref=src, dst_ref=dst, send_sem=send, recv_sem=recv,
            device_id=where, device_id_type=pl.DeviceIdType.MESH)

    def arrived(dst, recv):
        remote(dst, dst, recv, recv, seq=partner).wait_recv()

    def w_copy(zp):
        return pltpu.make_async_copy(
            w_ref.at[:, pl.ds(zp * feats, feats)], wv.at[zp], s_w.at[zp])

    def up_copy(zp):
        return remote(ogf.at[zp], ogf.at[zp], s_up.at[zp], r_z.at[zp], head=z + 1)

    def down_copy(zp):
        return remote(ogf.at[zp], ogf.at[zp], s_dn.at[zp], r_z.at[zp], head=z - 1)

    def kv_copy(o):
        if o == 0:
            src, dst, to = kc.at[:, pl.ds(0, leaf)], 1, partner
        elif o % 2 == 0:
            level = o.bit_length() - 1
            src = pb.at[:, pl.ds(leaf - (leaf >> (level - 1)), rows[o])]
            dst, to = o, flipped(me, o)
        else:
            src, dst, to = kc.at[:, pl.ds(starts[o - 1], rows[o])], o, partner
        slot = kc.at[:, pl.ds(starts[dst], rows[dst])]
        return remote(src, slot, s_kv.at[o], r_kv.at[dst], seq=to)

    def kv_arrived(o):
        arrived(kc.at[:, pl.ds(starts[o], rows[o])], r_kv.at[o])

    wide = seq_count // 2
    my_half = lax.div(me, jnp.int32(wide))

    def a_route(zp, j):
        to = jnp.int32(zp * per_shard + j)
        step = my_half - lax.div(to, jnp.int32(wide))
        return to, to + step * wide, step * step

    def a_copy(zp, j):
        to, dest, kind = a_route(zp, j)
        return remote(ogf.at[zp, :, pl.ds(j * kcols, kcols)], ogs.at[kind, me],
                      s_a.at[to], r_a.at[kind, me], seq=dest)

    def c_copy(o, n):
        part = pl.ds(n * (feats // 2), feats // 2)
        src, to = (0, flipped(me, o)) if o == 1 or o % 2 == 0 else (o - 1, partner)
        return remote(ctxs.at[src, part], ctxs.at[o, part], s_c.at[o, n], r_c.at[o, n], seq=to)

    def p_copy(g):
        return remote(dbuf.at[g, :, pl.ds(half, half)], pair.at[g], s_p.at[g], r_p.at[g],
                      seq=partner)

    def g_copy(g, o):
        return remote(dbuf.at[g, :, pl.ds(starts[o], rows[o])],
                      back.at[g, :, pl.ds(starts[o] - leaf, rows[o])],
                      s_g.at[g, o // 2], r_g.at[g, o // 2], seq=flipped(me, o))

    far = list(range(2, seq_count, 2))
    near = [o for o in far if o < wide]

    for zp in range(head_count):
        w_copy(zp).start()
    barrier = pltpu.get_barrier_semaphore()
    for o in range(1, seq_count):
        pl.semaphore_signal(barrier, inc=1, device_id={"seq": flipped(me, o)},
                            device_id_type=pl.DeviceIdType.MESH)

    @pl.when(z > 0)
    def _():
        pl.semaphore_signal(barrier, inc=1, device_id={"head": z - 1},
                            device_id_type=pl.DeviceIdType.MESH)

    @pl.when(z < head_count - 1)
    def _():
        pl.semaphore_signal(barrier, inc=1, device_id={"head": z + 1},
                            device_id_type=pl.DeviceIdType.MESH)

    ogf[z] = og_ref[...]
    kc[0, 0:leaf] = k_ref[...]
    kc[1, 0:leaf] = v_ref[...]
    for which, ref in enumerate((k_ref, v_ref)):
        for c in range(0, feats, 256):
            block = ref[:, c:c + 256]
            at = 0
            for level in range(1, levels):
                n = leaf >> level
                pool = jnp.where(
                    lax.broadcasted_iota(jnp.int32, (n, 2 * n), 1) // 2
                    == lax.broadcasted_iota(jnp.int32, (n, 2 * n), 0), 0.5, 0.0).astype(BF16)
                block = dot_nn(pool, block).astype(BF16)
                pb[which, at:at + n, c:c + 256] = block
                at += n
    inner = (z > 0) & (z < head_count - 1)

    @pl.when(inner)
    def _():
        pl.semaphore_wait(barrier, seq_count + 1)

    @pl.when(jnp.logical_not(inner))
    def _():
        pl.semaphore_wait(barrier, seq_count)

    @pl.when(z > 0)
    def _():
        down_copy(z).start()

    @pl.when(z < head_count - 1)
    def _():
        up_copy(z).start()

    kv_copy(0).start()
    for o in far:
        kv_copy(o).start()

    def scatter_grad(zp):
        for j in range(per_shard):
            _, dest, kind = a_route(zp, j)

            @pl.when(dest != me)
            def _():
                a_copy(zp, j).start()

            @pl.when(dest == me)
            def _():
                ogs[kind, me] = ogf[zp, :, j * kcols:(j + 1) * kcols]

    def project(zp, first=False):
        grad = ogf[zp]

        @pl.loop(0, feats // 256)
        def _(t):
            at = pl.ds(pl.multiple_of(t * 256, 256), 256)
            term = dot_nt(wv[zp, at], grad)
            cga[at] = term if first else cga[at] + term

    def gather_step(k):
        @pl.when(z >= k)
        def _():
            zp = z - k
            arrived(ogf.at[zp], r_z.at[zp])

            @pl.when(z < head_count - 1)
            def _():
                up_copy(zp).start()

        @pl.when(z + k < head_count)
        def _():
            zp = z + k
            arrived(ogf.at[zp], r_z.at[zp])

            @pl.when(z > 0)
            def _():
                down_copy(zp).start()

        @pl.when(z >= k)
        def _():
            scatter_grad(z - k)
            project(z - k)

        @pl.when(z + k < head_count)
        def _():
            scatter_grad(z + k)
            project(z + k)

    scatter_grad(z)
    for zp in range(head_count):
        w_copy(zp).wait()
    project(z, first=True)
    gather_step(1)

    for o in far:
        kv_arrived(o)
        kv_copy(o + 1).start()
    kv_arrived(1)
    for o in far:
        kv_arrived(o + 1)

    log2e = 1.4426950408889634
    my_doc = doc[0, me]
    biases = []
    for o in sorted(starts, key=lambda p: starts[p]):
        level = float(max(o.bit_length() - 1, 0))
        same = doc[0, flipped(me, o)] == my_doc
        biases.append((starts[o], rows[o], jnp.where(same, level, -1e30).astype(F32)))

    def forward(first, last):
        @pl.loop(first, last)
        def _(h):
            at = pl.ds(pl.multiple_of(h * DH, DH), DH)
            keys, vals, query = kc[0, :, at], kc[1, :, at], q_ref[:, at]
            raw = dot_nt(keys, query)
            shifted = jnp.concatenate(
                [raw[s:s + n] * (scaling * log2e) + b for s, n, b in biases], axis=0)
            top = jnp.max(shifted, axis=0, keepdims=True)
            weights = jnp.exp2(shifted - top)
            inv = 1.0 / jnp.sum(weights, axis=0, keepdims=True)
            prob = (weights * inv).astype(BF16)
            probs[h] = prob
            out = dot_tn(vals, prob)
            ctxs[0, at] = out.astype(BF16)
            ctx_out[:, at] = out.T.astype(BF16)

    forward(0, heads // 2)
    for o in near + [1]:
        c_copy(o, 0).start()
    if head_count > 2:
        gather_step(2)
    forward(heads // 2, heads)
    for o in near + [1]:
        c_copy(o, 1).start()
    for k in range(3, head_count):
        gather_step(k)
    cgt[...] = cga[...].astype(BF16)

    def finish(g):
        arrived(pair.at[g], r_p.at[g])
        for which in range(2):
            dbuf[g, which, leaf:half] = (
                dbuf[g, which, leaf:half].astype(F32) + pair[g, which, leaf:half].astype(F32)
            ).astype(BF16)
        for o in far:
            g_copy(g, o).start()

    @pl.loop(0, groups)
    def _(g):
        for i in range(GROUP_HEADS):
            h = g * GROUP_HEADS + i
            at = pl.ds(pl.multiple_of(h * DH, DH), DH)
            lanes = slice(i * DH, (i + 1) * DH)
            keys, vals, query = kc[0, :, at], kc[1, :, at], q_ref[:, at]
            grad = cgt[at]
            prob = probs[h]
            delta = jnp.sum(grad.astype(F32) * ctxs[0, at].astype(F32), axis=0, keepdims=True)
            prob_grad = dot_nn(vals, grad)
            score_grad = (prob.astype(F32) * (prob_grad - delta)).astype(BF16)
            dq_out[:, at] = (dot_tn(keys, score_grad) * scaling).T.astype(BF16)
            dk = dot_nn(score_grad, query) * scaling
            dv = dot_nt(prob, grad)
            for which, full in enumerate((dk, dv)):
                own[g, which, :, lanes] = full[:leaf]
                dbuf[g, which, leaf:, lanes] = full[leaf:].astype(BF16)
        p_copy(g).start()

        @pl.when(g > 0)
        def _():
            finish(g - 1)

    finish(groups - 1)

    for o in near:
        for n in range(2):
            c_copy(o, n).wait_recv()
            c_copy(o + 1, n).start()

    def share(kind, first):
        for n, o in enumerate([0, 1] + near + [o + 1 for o in near]):
            if o % 2 == 1 and first:
                for part in range(2):
                    c_copy(o, part).wait_recv()
            src = flipped(me, o)
            if o:
                arrived(ogs.at[kind, src], r_a.at[kind, src])
            grad = ogs[kind, src]

            @pl.loop(0, feats // 256)
            def _(t):
                at = pl.ds(pl.multiple_of(t * 256, 256), 256)
                term = dot_nn(ctxs[o, at], grad)
                acc[at] = term if n == 0 else acc[at] + term

    sum_copy = remote(sums.at[0], sums.at[1], s_s.at[0], r_s.at[0], seq=flipped(me, wide))
    share(1, True)
    sums[0] = acc[...].astype(BF16)
    sum_copy.start()
    share(0, False)

    far_rows = half - leaf
    r_id = lax.broadcasted_iota(jnp.int32, (leaf, far_rows), 0)
    c_id = lax.broadcasted_iota(jnp.int32, (leaf, far_rows), 1)
    spread = jnp.zeros((leaf, far_rows), F32)
    for o in far:
        level = o.bit_length() - 1
        hit = (lax.shift_right_logical(r_id, level) == c_id - (starts[o] - leaf))
        spread = jnp.where(hit, 0.5 ** level, spread)
    spread = spread.astype(BF16)
    for g in range(groups):
        for o in far:
            arrived(back.at[g, :, pl.ds(starts[o] - leaf, rows[o])], r_g.at[g, o // 2])
        for which, out in enumerate((dk_out, dv_out)):
            total = own[g, which] + pair[g, which, :leaf].astype(F32) + dot_nn(
                spread, back[g, which])
            out[:, g * gcols:(g + 1) * gcols] = total.astype(BF16)

    sum_copy.wait()
    wg_out[...] = (acc[...] + sums[1].astype(F32)).astype(BF16)

    for zp in range(head_count):
        @pl.when((z < head_count - 1) & (zp <= z))
        def _():
            up_copy(zp).wait_send()

        @pl.when((z > 0) & (zp >= z))
        def _():
            down_copy(zp).wait_send()

        for j in range(per_shard):
            @pl.when(a_route(zp, j)[1] != me)
            def _():
                a_copy(zp, j).wait_send()
    kv_copy(0).wait_send()
    for o in far:
        kv_copy(o).wait_send()
        kv_copy(o + 1).wait_send()
    for o in range(1, wide):
        for n in range(2):
            c_copy(o, n).wait_send()
    for g in range(groups):
        p_copy(g).wait_send()
        for o in far:
            g_copy(g, o).wait_send()


def copy_kernel(*refs):
    count = len(refs) // 2
    for i in range(count):
        refs[count + i][...] = refs[i][...]


def local(queries, keys, values, out_weight, out_grad, block_doc):
    seq_count, head_count = lax.axis_size("seq"), lax.axis_size("head")
    _, leaf, feats = queries.shape
    model = out_weight.shape[1]
    _, _, cols = pieces_of(seq_count, leaf)
    half = cols // 2
    heads = feats // DH
    gcols = GROUP_HEADS * DH
    groups = feats // gcols
    kcols = model // seq_count
    dma = pltpu.SemaphoreType.DMA
    vmem = pl.BlockSpec(memory_space=pltpu.VMEM)
    block = jax.ShapeDtypeStruct((leaf, feats), BF16)
    results = pl.pallas_call(
        functools.partial(kernel, seq_count, head_count, leaf, feats),
        out_shape=[block] * 4 + [jax.ShapeDtypeStruct((feats, kcols), BF16)],
        in_specs=[pl.BlockSpec(memory_space=pltpu.SMEM)] + [vmem] * 4
        + [pl.BlockSpec(memory_space=pl.ANY)],
        out_specs=[vmem] * 5,
        scratch_shapes=[
            pltpu.VMEM((head_count, feats, feats), BF16),
            pltpu.VMEM((head_count, leaf, feats), BF16),
            pltpu.VMEM((2, cols, feats), BF16),
            pltpu.VMEM((2, leaf, feats), BF16),
            pltpu.VMEM((heads, cols, leaf), BF16),
            pltpu.VMEM((seq_count // 2, feats, leaf), BF16),
            pltpu.VMEM((2, seq_count, leaf, kcols), BF16),
            pltpu.VMEM((feats, leaf), F32),
            pltpu.VMEM((feats, leaf), BF16),
            pltpu.VMEM((groups, 2, leaf, gcols), F32),
            pltpu.VMEM((groups, 2, cols, gcols), BF16),
            pltpu.VMEM((groups, 2, half, gcols), BF16),
            pltpu.VMEM((groups, 2, half - leaf, gcols), BF16),
            pltpu.VMEM((feats, kcols), F32),
            dma((head_count,)), dma((head_count,)), dma((head_count,)), dma((head_count,)),
            dma((seq_count,)), dma((seq_count,)), dma((seq_count,)), dma((2, seq_count)),
            dma((seq_count, 2)), dma((seq_count, 2)), dma((groups,)), dma((groups,)),
            dma((groups, seq_count // 2)), dma((groups, seq_count // 2)),
            pltpu.VMEM((2, feats, kcols), BF16), dma((1,)), dma((1,)),
        ],
        compiler_params=pltpu.CompilerParams(
            collective_id=0, has_side_effects=True, vmem_limit_bytes=60 * 1024 * 1024),
        cost_estimate=pl.CostEstimate(
            flops=8 * 10**9, bytes_accessed=16 * 2**20, transcendentals=2 * 2**20),
        name="hier_attention",
    )(block_doc, queries[0], keys[0], values[0], out_grad[0], out_weight)
    steps = 4
    tiles = [pl.BlockSpec((r.shape[0] // steps, r.shape[1]), lambda i: (i, 0)) for r in results]
    context, query_grad, key_grad, value_grad, weight_grad = pl.pallas_call(
        copy_kernel,
        grid=(steps,),
        out_shape=[jax.ShapeDtypeStruct(r.shape, r.dtype) for r in results],
        in_specs=tiles,
        out_specs=tiles,
        compiler_params=pltpu.CompilerParams(vmem_limit_bytes=60 * 1024 * 1024),
        name="hand_over",
    )(*results)
    return context[None], query_grad[None], key_grad[None], value_grad[None], weight_grad


def solution(mesh):
    blocks = P(None, "seq", "head")
    return jax.shard_map(
        local,
        mesh=mesh,
        in_specs=(blocks, blocks, blocks, P("head", None), blocks, P()),
        out_specs=(blocks, blocks, blocks, blocks, P("head", "seq")),
        check_vma=False,
    )
```

```python
import functools
import math

import jax
import jax.numpy as jnp
from jax import lax
from jax.experimental import pallas as pl
from jax.experimental.pallas import tpu as pltpu
from jax.sharding import PartitionSpec as P

DH = 128
GROUP_HEADS = 2
F32 = jnp.float32
BF16 = jnp.bfloat16


def flipped(index, mask):
    out = index
    bit = 1
    while bit <= mask:
        if mask & bit:
            out = out + (1 - 2 * lax.rem(lax.div(index, jnp.int32(bit)), jnp.int32(2))) * bit
        bit *= 2
    return out


def dot_nn(a, b):
    return lax.dot_general(a, b, (((1,), (0,)), ((), ())), preferred_element_type=F32)


def dot_nt(a, b):
    return lax.dot_general(a, b, (((1,), (1,)), ((), ())), preferred_element_type=F32)


def dot_tn(a, b):
    return lax.dot_general(a, b, (((0,), (0,)), ((), ())), preferred_element_type=F32)


def pieces_of(seq_count, leaf):
    rows, starts, at = {}, {}, 0
    for parity in (0, 1):
        for o in range(parity, seq_count, 2):
            level = max(o.bit_length() - 1, 0)
            rows[o], starts[o] = leaf >> level, at
            at += rows[o]
    return rows, starts, at


def kernel(seq_count, head_count, leaf, feats,
           doc, q_ref, k_ref, v_ref, og_ref, w_ref,
           ctx_out, dq_out, dk_out, dv_out, wg_out,
           wv, ogf, kc, pb, probs, ctxs, ogs, cga, cgt, own, dbuf, pair, back, acc,
           s_w, s_up, s_dn, r_z, s_kv, r_kv, s_a, r_a, s_c, r_c, s_p, r_p, s_g, r_g, sums, s_s, r_s):
    me = lax.axis_index("seq")
    z = lax.axis_index("head")
    partner = flipped(me, 1)
    levels = seq_count.bit_length() - 1
    rows, starts, cols = pieces_of(seq_count, leaf)
    half = cols // 2
    heads = feats // DH
    gcols = GROUP_HEADS * DH
    groups = feats // gcols
    per_shard = seq_count // head_count
    kcols = feats // per_shard
    scaling = 1.0 / math.sqrt(DH)

    def remote(src, dst, send, recv, **where):
        return pltpu.make_async_remote_copy(
            src_ref=src, dst_ref=dst, send_sem=send, recv_sem=recv,
            device_id=where, device_id_type=pl.DeviceIdType.MESH)

    def arrived(dst, recv):
        remote(dst, dst, recv, recv, seq=partner).wait_recv()

    def w_copy(zp):
        return pltpu.make_async_copy(
            w_ref.at[:, pl.ds(zp * feats, feats)], wv.at[zp], s_w.at[zp])

    def up_copy(zp):
        return remote(ogf.at[zp], ogf.at[zp], s_up.at[zp], r_z.at[zp], head=z + 1)

    def down_copy(zp):
        return remote(ogf.at[zp], ogf.at[zp], s_dn.at[zp], r_z.at[zp], head=z - 1)

    def kv_copy(o):
        if o == 0:
            src, dst, to = kc.at[:, pl.ds(0, leaf)], 1, partner
        elif o % 2 == 0:
            level = o.bit_length() - 1
            src = pb.at[:, pl.ds(leaf - (leaf >> (level - 1)), rows[o])]
            dst, to = o, flipped(me, o)
        else:
            src, dst, to = kc.at[:, pl.ds(starts[o - 1], rows[o])], o, partner
        slot = kc.at[:, pl.ds(starts[dst], rows[dst])]
        return remote(src, slot, s_kv.at[o], r_kv.at[dst], seq=to)

    def kv_arrived(o):
        arrived(kc.at[:, pl.ds(starts[o], rows[o])], r_kv.at[o])

    wide = seq_count // 2
    my_half = lax.div(me, jnp.int32(wide))

    def a_route(zp, j):
        to = jnp.int32(zp * per_shard + j)
        step = my_half - lax.div(to, jnp.int32(wide))
        return to, to + step * wide, step * step

    def a_copy(zp, j):
        to, dest, kind = a_route(zp, j)
        return remote(ogf.at[zp, :, pl.ds(j * kcols, kcols)], ogs.at[kind, me],
                      s_a.at[to], r_a.at[kind, me], seq=dest)

    def c_copy(o, n):
        part = pl.ds(n * (feats // 2), feats // 2)
        src, to = (0, flipped(me, o)) if o == 1 or o % 2 == 0 else (o - 1, partner)
        return remote(ctxs.at[src, part], ctxs.at[o, part], s_c.at[o, n], r_c.at[o, n], seq=to)

    def p_copy(g):
        return remote(dbuf.at[g, :, pl.ds(half, half)], pair.at[g], s_p.at[g], r_p.at[g],
                      seq=partner)

    def g_copy(g, o):
        return remote(dbuf.at[g, :, pl.ds(starts[o], rows[o])],
                      back.at[g, :, pl.ds(starts[o] - leaf, rows[o])],
                      s_g.at[g, o // 2], r_g.at[g, o // 2], seq=flipped(me, o))

    far = list(range(2, seq_count, 2))
    near = [o for o in far if o < wide]

    for zp in range(head_count):
        w_copy(zp).start()
    barrier = pltpu.get_barrier_semaphore()
    for o in range(1, seq_count):
        pl.semaphore_signal(barrier, inc=1, device_id={"seq": flipped(me, o)},
                            device_id_type=pl.DeviceIdType.MESH)

    @pl.when(z > 0)
    def _():
        pl.semaphore_signal(barrier, inc=1, device_id={"head": z - 1},
                            device_id_type=pl.DeviceIdType.MESH)

    @pl.when(z < head_count - 1)
    def _():
        pl.semaphore_signal(barrier, inc=1, device_id={"head": z + 1},
                            device_id_type=pl.DeviceIdType.MESH)

    ogf[z] = og_ref[...]
    kc[0, 0:leaf] = k_ref[...]
    kc[1, 0:leaf] = v_ref[...]
    for which, ref in enumerate((k_ref, v_ref)):
        for c in range(0, feats, 256):
            block = ref[:, c:c + 256]
            at = 0
            for level in range(1, levels):
                n = leaf >> level
                pool = jnp.where(
                    lax.broadcasted_iota(jnp.int32, (n, 2 * n), 1) // 2
                    == lax.broadcasted_iota(jnp.int32, (n, 2 * n), 0), 0.5, 0.0).astype(BF16)
                block = dot_nn(pool, block).astype(BF16)
                pb[which, at:at + n, c:c + 256] = block
                at += n
    inner = (z > 0) & (z < head_count - 1)

    @pl.when(inner)
    def _():
        pl.semaphore_wait(barrier, seq_count + 1)

    @pl.when(jnp.logical_not(inner))
    def _():
        pl.semaphore_wait(barrier, seq_count)

    @pl.when(z > 0)
    def _():
        down_copy(z).start()

    @pl.when(z < head_count - 1)
    def _():
        up_copy(z).start()

    kv_copy(0).start()
    for o in far:
        kv_copy(o).start()

    def scatter_grad(zp):
        for j in range(per_shard):
            _, dest, kind = a_route(zp, j)

            @pl.when(dest != me)
            def _():
                a_copy(zp, j).start()

            @pl.when(dest == me)
            def _():
                ogs[kind, me] = ogf[zp, :, j * kcols:(j + 1) * kcols]

    def project(zp, first=False):
        grad = ogf[zp]

        @pl.loop(0, feats // 256)
        def _(t):
            at = pl.ds(pl.multiple_of(t * 256, 256), 256)
            term = dot_nt(wv[zp, at], grad)
            cga[at] = term if first else cga[at] + term

    def gather_step(k):
        @pl.when(z >= k)
        def _():
            zp = z - k
            arrived(ogf.at[zp], r_z.at[zp])

            @pl.when(z < head_count - 1)
            def _():
                up_copy(zp).start()

        @pl.when(z + k < head_count)
        def _():
            zp = z + k
            arrived(ogf.at[zp], r_z.at[zp])

            @pl.when(z > 0)
            def _():
                down_copy(zp).start()

        @pl.when(z >= k)
        def _():
            scatter_grad(z - k)
            project(z - k)

        @pl.when(z + k < head_count)
        def _():
            scatter_grad(z + k)
            project(z + k)

    scatter_grad(z)
    for zp in range(head_count):
        w_copy(zp).wait()
    project(z, first=True)
    gather_step(1)

    for o in far:
        kv_arrived(o)
        kv_copy(o + 1).start()
    kv_arrived(1)
    for o in far:
        kv_arrived(o + 1)

    log2e = 1.4426950408889634
    my_doc = doc[0, me]
    biases = []
    for o in sorted(starts, key=lambda p: starts[p]):
        level = float(max(o.bit_length() - 1, 0))
        same = doc[0, flipped(me, o)] == my_doc
        biases.append((starts[o], rows[o], jnp.where(same, level, -1e30).astype(F32)))

    def forward(first, last):
        @pl.loop(first, last)
        def _(h):
            at = pl.ds(pl.multiple_of(h * DH, DH), DH)
            keys, vals, query = kc[0, :, at], kc[1, :, at], q_ref[:, at]
            raw = dot_nt(keys, query)
            shifted = jnp.concatenate(
                [raw[s:s + n] * (scaling * log2e) + b for s, n, b in biases], axis=0)
            top = jnp.max(shifted, axis=0, keepdims=True)
            weights = jnp.exp2(shifted - top)
            inv = 1.0 / jnp.sum(weights, axis=0, keepdims=True)
            prob = (weights * inv).astype(BF16)
            probs[h] = prob
            out = dot_tn(vals, prob)
            ctxs[0, at] = out.astype(BF16)
            ctx_out[:, at] = out.T.astype(BF16)

    forward(0, heads // 2)
    for o in near + [1]:
        c_copy(o, 0).start()
    if head_count > 2:
        gather_step(2)
    forward(heads // 2, heads)
    for o in near + [1]:
        c_copy(o, 1).start()
    for k in range(3, head_count):
        gather_step(k)
    cgt[...] = cga[...].astype(BF16)

    def finish(g):
        arrived(pair.at[g], r_p.at[g])
        for which in range(2):
            dbuf[g, which, leaf:half] = (
                dbuf[g, which, leaf:half].astype(F32) + pair[g, which, leaf:half].astype(F32)
            ).astype(BF16)
        for o in far:
            g_copy(g, o).start()

    def share(kind, first):
        for n, o in enumerate([0, 1] + near + [o + 1 for o in near]):
            if o % 2 == 1 and first:
                for part in range(2):
                    c_copy(o, part).wait_recv()
            src = flipped(me, o)
            if o:
                arrived(ogs.at[kind, src], r_a.at[kind, src])
            grad = ogs[kind, src]

            @pl.loop(0, feats // 256)
            def _(t):
                at = pl.ds(pl.multiple_of(t * 256, 256), 256)
                term = dot_nn(ctxs[o, at], grad)
                acc[at] = term if n == 0 else acc[at] + term

    def backward(g):
        for i in range(GROUP_HEADS):
            h = g * GROUP_HEADS + i
            at = pl.ds(pl.multiple_of(h * DH, DH), DH)
            lanes = slice(i * DH, (i + 1) * DH)
            keys, vals, query = kc[0, :, at], kc[1, :, at], q_ref[:, at]
            grad = cgt[at]
            prob = probs[h]
            delta = jnp.sum(grad.astype(F32) * ctxs[0, at].astype(F32), axis=0, keepdims=True)
            prob_grad = dot_nn(vals, grad)
            score_grad = (prob.astype(F32) * (prob_grad - delta)).astype(BF16)
            dq_out[:, at] = (dot_tn(keys, score_grad) * scaling).T.astype(BF16)
            dk = dot_nn(score_grad, query) * scaling
            dv = dot_nt(prob, grad)
            for which, full in enumerate((dk, dv)):
                own[g, which, :, lanes] = full[:leaf]
                dbuf[g, which, leaf:, lanes] = full[leaf:].astype(BF16)
        p_copy(g).start()

        @pl.when(g > 0)
        def _():
            finish(g - 1)

    pl.loop(0, groups // 2)(backward)
    for o in near:
        for n in range(2):
            c_copy(o, n).wait_recv()
            c_copy(o + 1, n).start()

    sum_copy = remote(sums.at[0], sums.at[1], s_s.at[0], r_s.at[0], seq=flipped(me, wide))
    share(1, True)
    sums[0] = acc[...].astype(BF16)
    sum_copy.start()
    pl.loop(groups // 2, groups)(backward)
    finish(groups - 1)

    share(0, False)

    far_rows = half - leaf
    r_id = lax.broadcasted_iota(jnp.int32, (leaf, far_rows), 0)
    c_id = lax.broadcasted_iota(jnp.int32, (leaf, far_rows), 1)
    spread = jnp.zeros((leaf, far_rows), F32)
    for o in far:
        level = o.bit_length() - 1
        hit = (lax.shift_right_logical(r_id, level) == c_id - (starts[o] - leaf))
        spread = jnp.where(hit, 0.5 ** level, spread)
    spread = spread.astype(BF16)
    for g in range(groups):
        for o in far:
            arrived(back.at[g, :, pl.ds(starts[o] - leaf, rows[o])], r_g.at[g, o // 2])
        for which, out in enumerate((dk_out, dv_out)):
            total = own[g, which] + pair[g, which, :leaf].astype(F32) + dot_nn(
                spread, back[g, which])
            out[:, g * gcols:(g + 1) * gcols] = total.astype(BF16)

    sum_copy.wait()
    wg_out[...] = (acc[...] + sums[1].astype(F32)).astype(BF16)

    for zp in range(head_count):
        @pl.when((z < head_count - 1) & (zp <= z))
        def _():
            up_copy(zp).wait_send()

        @pl.when((z > 0) & (zp >= z))
        def _():
            down_copy(zp).wait_send()

        for j in range(per_shard):
            @pl.when(a_route(zp, j)[1] != me)
            def _():
                a_copy(zp, j).wait_send()
    kv_copy(0).wait_send()
    for o in far:
        kv_copy(o).wait_send()
        kv_copy(o + 1).wait_send()
    for o in range(1, wide):
        for n in range(2):
            c_copy(o, n).wait_send()
    for g in range(groups):
        p_copy(g).wait_send()
        for o in far:
            g_copy(g, o).wait_send()


def copy_kernel(*refs):
    count = len(refs) // 2
    for i in range(count):
        refs[count + i][...] = refs[i][...]


def local(queries, keys, values, out_weight, out_grad, block_doc):
    seq_count, head_count = lax.axis_size("seq"), lax.axis_size("head")
    _, leaf, feats = queries.shape
    model = out_weight.shape[1]
    _, _, cols = pieces_of(seq_count, leaf)
    half = cols // 2
    heads = feats // DH
    gcols = GROUP_HEADS * DH
    groups = feats // gcols
    kcols = model // seq_count
    dma = pltpu.SemaphoreType.DMA
    vmem = pl.BlockSpec(memory_space=pltpu.VMEM)
    block = jax.ShapeDtypeStruct((leaf, feats), BF16)
    results = pl.pallas_call(
        functools.partial(kernel, seq_count, head_count, leaf, feats),
        out_shape=[block] * 4 + [jax.ShapeDtypeStruct((feats, kcols), BF16)],
        in_specs=[pl.BlockSpec(memory_space=pltpu.SMEM)] + [vmem] * 4
        + [pl.BlockSpec(memory_space=pl.ANY)],
        out_specs=[vmem] * 5,
        scratch_shapes=[
            pltpu.VMEM((head_count, feats, feats), BF16),
            pltpu.VMEM((head_count, leaf, feats), BF16),
            pltpu.VMEM((2, cols, feats), BF16),
            pltpu.VMEM((2, leaf, feats), BF16),
            pltpu.VMEM((heads, cols, leaf), BF16),
            pltpu.VMEM((seq_count // 2, feats, leaf), BF16),
            pltpu.VMEM((2, seq_count, leaf, kcols), BF16),
            pltpu.VMEM((feats, leaf), F32),
            pltpu.VMEM((feats, leaf), BF16),
            pltpu.VMEM((groups, 2, leaf, gcols), F32),
            pltpu.VMEM((groups, 2, cols, gcols), BF16),
            pltpu.VMEM((groups, 2, half, gcols), BF16),
            pltpu.VMEM((groups, 2, half - leaf, gcols), BF16),
            pltpu.VMEM((feats, kcols), F32),
            dma((head_count,)), dma((head_count,)), dma((head_count,)), dma((head_count,)),
            dma((seq_count,)), dma((seq_count,)), dma((seq_count,)), dma((2, seq_count)),
            dma((seq_count, 2)), dma((seq_count, 2)), dma((groups,)), dma((groups,)),
            dma((groups, seq_count // 2)), dma((groups, seq_count // 2)),
            pltpu.VMEM((2, feats, kcols), BF16), dma((1,)), dma((1,)),
        ],
        compiler_params=pltpu.CompilerParams(
            collective_id=0, has_side_effects=True, vmem_limit_bytes=60 * 1024 * 1024),
        cost_estimate=pl.CostEstimate(
            flops=8 * 10**9, bytes_accessed=16 * 2**20, transcendentals=2 * 2**20),
        name="hier_attention",
    )(block_doc, queries[0], keys[0], values[0], out_grad[0], out_weight)
    steps = 4
    tiles = [pl.BlockSpec((r.shape[0] // steps, r.shape[1]), lambda i: (i, 0)) for r in results]
    context, query_grad, key_grad, value_grad, weight_grad = pl.pallas_call(
        copy_kernel,
        grid=(steps,),
        out_shape=[jax.ShapeDtypeStruct(r.shape, r.dtype) for r in results],
        in_specs=tiles,
        out_specs=tiles,
        compiler_params=pltpu.CompilerParams(vmem_limit_bytes=60 * 1024 * 1024),
        name="hand_over",
    )(*results)
    return context[None], query_grad[None], key_grad[None], value_grad[None], weight_grad


def solution(mesh):
    blocks = P(None, "seq", "head")
    return jax.shard_map(
        local,
        mesh=mesh,
        in_specs=(blocks, blocks, blocks, P("head", None), blocks, P()),
        out_specs=(blocks, blocks, blocks, blocks, P("head", "seq")),
        check_vma=False,
    )
```
